256 devices in a mesh: leaf: 64 (over x, z, core), rhs: 4 (over y).
Axes of the slice: x: 4, y: 4, z: 8, core: 2. Of those that a mesh axis runs over, the one named last changes fastest.
Arguments:
- points: float32 [8, 262144], P(None, 'leaf'), may hold values from -6 to 6
- charges: bfloat16 [262144, 512], P('leaf', 'rhs'), may hold values from -6 to 6
- tree_order: int32 [262144], P('leaf'), may hold values from 0 to 262143, as said below
- leaf_basis: bfloat16 [1024, 256, 128], P('leaf'), may hold values from -0.375 to 0.375
- local_transfer: bfloat16 [1984, 128, 128], P('leaf'), may hold values from -0.4375 to 0.4375
- local_coupling: bfloat16 [960, 128, 128], P('leaf'), may hold values from -0.5 to 0.5
- top_transfer: bfloat16 [62, 128, 128], replicated, may hold values from -0.4375 to 0.4375
- top_coupling: bfloat16 [63, 128, 128], replicated, may hold values from -0.5 to 0.5
Outputs:
- potential: float32 [262144, 512], P('leaf', 'rhs')
The draws below stay inside these ranges and needn't reach their ends.
Inputs may be any that keep to these rules, and one draw needn't show every extreme that they name: `tree_order`: each block of 256 consecutive positions (one leaf) holds each point of that same block exactly once.
All inputs are finite; a program needn't handle non-finite values.
Results may differ from the reference program's by a relative error of at most 0.0025.
Values may be sent and summed in bfloat16 or wider, within the bound.
A program may use at most 128 MiB of HBM per device.

```python
import jax
import jax.numpy as jnp
from jax import lax

LEAF_SIZE = 256
RANK = 128
DIMS = 8
RHS = 512
LEAF_DEV = 16
LEAVES = 1024
POINTS = 262144
LOCAL_NODES = 1984
LOCAL_PAIRS = 960
TOP_NODES = 62
TOP_PAIRS = 63
N_LEAF = 64


def draw_tree_order(key, part):
    key = jax.random.fold_in(key, 7)
    keys = jax.random.split(key, LEAVES)
    orders = jax.vmap(lambda sub: jax.random.permutation(sub, LEAF_SIZE))(keys)
    starts = jnp.arange(LEAVES, dtype=jnp.int32)[:, None] * LEAF_SIZE
    return (orders.astype(jnp.int32) + starts).reshape(-1)


def shard_levels(stream_key, extent, cuts, low, high):
    level, own = 1.0, jax.random.fold_in(stream_key, 6)
    for position, shards_of in cuts:
        draws = jnp.exp(jax.random.uniform(jax.random.fold_in(own, position), (shards_of,), jnp.float32, low / len(cuts), high / len(cuts)))
        level = level * jnp.repeat(draws, extent[position] // shards_of).reshape([-1 if axis == position else 1 for axis in range(len(extent))])
    return level


def centred(own_key, shape, deviation, bound, shards=(), kind=jnp.bfloat16):
    entries = deviation * jax.random.normal(own_key, shape, jnp.float32)
    if shards:
        entries = entries * shard_levels(own_key, shape, shards, -0.22, 0.18)
    return jnp.clip(entries, -bound, bound).astype(kind)


def setup_inputs(seed: int = 0) -> dict:
    arg_keys = jax.random.split(jax.random.key(seed), 9)
    points = centred(arg_keys[0], (DIMS, POINTS), 1.0, 6.0, ((1, 64),), jnp.float32)
    charges = centred(arg_keys[1], (POINTS, RHS), 1.0, 6.0, ((0, 64), (1, 4)))
    tree_order = draw_tree_order(jax.random.fold_in(arg_keys[8], 71), 0)
    leaf_basis = centred(arg_keys[3], (LEAVES, LEAF_SIZE, RANK), LEAF_SIZE ** -0.5, 0.375, ((0, 64),))
    local_transfer = centred(arg_keys[4], (LOCAL_NODES, RANK, RANK), (RANK * 1414 // 1000) ** -0.5, 0.4375, ((0, 64),))
    local_coupling = centred(arg_keys[5], (LOCAL_PAIRS, RANK, RANK), RANK ** -0.5, 0.5, ((0, 64),))
    top_transfer = centred(arg_keys[6], (TOP_NODES, RANK, RANK), (RANK * 1414 // 1000) ** -0.5, 0.4375)
    top_coupling = centred(arg_keys[7], (TOP_PAIRS, RANK, RANK), RANK ** -0.5, 0.5)
    return dict(points=points, charges=charges, tree_order=tree_order, leaf_basis=leaf_basis, local_transfer=local_transfer, local_coupling=local_coupling, top_transfer=top_transfer, top_coupling=top_coupling)


KERNEL_RATE = 0.1
RIDGE_SHIFT = 0.5


def kernel_blocks(coords):
    width = coords.shape[2]
    total = jnp.zeros((coords.shape[0], width, width), jnp.float32)
    for column in range(coords.shape[1]):
        spread = coords[:, column, :, None] - coords[:, column, None, :]
        total = total + spread * spread
    blocks = jnp.exp(-KERNEL_RATE * total) + RIDGE_SHIFT * jnp.eye(width, dtype=jnp.float32)
    return blocks.astype(jnp.bfloat16)


def reference(points, charges, tree_order, leaf_basis, local_transfer, local_coupling, top_transfer, top_coupling):
    high = lax.Precision.HIGHEST
    leaves = LEAVES
    per_dev = LEAF_DEV
    groups = N_LEAF
    ordered = charges[tree_order].reshape(leaves, LEAF_SIZE, RHS)
    coords = points[:, tree_order].reshape(DIMS, leaves, LEAF_SIZE).transpose(1, 0, 2)

    def leaf_apply(pieces):
        block_coords, values = pieces
        blocks = kernel_blocks(block_coords)
        return jnp.einsum('lpq,lqc->lpc', blocks.astype(jnp.float32), values.astype(jnp.float32), precision=high)

    direct = lax.map(leaf_apply, (coords.reshape(groups, per_dev, DIMS, LEAF_SIZE), ordered.reshape(groups, per_dev, LEAF_SIZE, RHS)))
    direct = direct.reshape(leaves, LEAF_SIZE, RHS)
    basis = leaf_basis.astype(jnp.float32)
    first_up = jnp.einsum('lpr,lpc->lrc', basis, ordered.astype(jnp.float32), precision=high)
    low_levels = per_dev.bit_length() - 1
    top_levels = groups.bit_length() - 1
    total_levels = low_levels + top_levels
    local_t = local_transfer.reshape(groups, 2 * per_dev - 1, RANK, RANK)
    local_c = local_coupling.reshape(groups, per_dev - 1, RANK, RANK)

    def transfer_at(height):
        if height <= low_levels:
            count = per_dev >> height
            offset = 2 * per_dev - 2 * count
            return local_t[:, offset:offset + count].reshape(groups * count, RANK, RANK).astype(jnp.float32)
        upper = height - low_levels
        offset = groups - (groups >> (upper - 1))
        return top_transfer[offset:offset + (groups >> upper)].astype(jnp.float32)

    def coupling_at(height):
        if height < low_levels:
            count = per_dev >> (height + 1)
            offset = per_dev - (per_dev >> height)
            return local_c[:, offset:offset + count].reshape(groups * count, RANK, RANK).astype(jnp.float32)
        upper = height - low_levels
        offset = groups - (groups >> upper)
        return top_coupling[offset:offset + (groups >> (upper + 1))].astype(jnp.float32)

    upward = [first_up]
    for height in range(total_levels):
        projected = jnp.einsum('nrs,nrc->nsc', transfer_at(height), upward[height], precision=high)
        upward.append(projected[0::2] + projected[1::2])
    sides = []
    for height in range(total_levels):
        mats = coupling_at(height)
        nodes = upward[height]
        to_left = jnp.einsum('nrs,nsc->nrc', mats, nodes[1::2], precision=high)
        to_right = jnp.einsum('nsr,nsc->nrc', mats, nodes[0::2], precision=high)
        sides.append(jnp.stack((to_left, to_right), axis=1).reshape(nodes.shape))
    above = jnp.zeros((1, RANK, RHS), jnp.float32)
    for height in reversed(range(total_levels)):
        spread_down = jnp.einsum('nrs,nsc->nrc', transfer_at(height), jnp.repeat(above, 2, axis=0), precision=high)
        above = sides[height] + spread_down
    final = direct + jnp.einsum('lpr,lrc->lpc', basis, above, precision=high)
    result = jnp.zeros((POINTS, RHS), jnp.float32)
    return result.at[tree_order].set(final.reshape(POINTS, RHS))
```

```python
import functools
import math

import jax
import jax.numpy as jnp
from jax import lax
from jax.experimental import pallas as pl
from jax.experimental.pallas import tpu as pltpu
from jax.sharding import PartitionSpec as P

MESH = pl.DeviceIdType.MESH
BF, F32 = jnp.bfloat16, jnp.float32
LEAF, RANK, COLS, LEAVES = 256, 128, 128, 16
HALF = COLS // 2
NZ, NX = 8, 4
SCALE = math.sqrt(0.1 * math.log2(math.e))
CHUNK = 4


def nn(a, b):
    return lax.dot_general(a, b, (((1,), (0,)), ((), ())), preferred_element_type=F32)


def nt(a, b):
    return lax.dot_general(a, b, (((1,), (1,)), ((), ())), preferred_element_type=F32)


def tn(a, b):
    return lax.dot_general(a, b, (((0,), (0,)), ((), ())), preferred_element_type=F32)


def split(u):
    hi = u.astype(BF)
    return hi, (u - hi.astype(F32)).astype(BF)


def times(u, mat):
    hi, lo = split(u)
    return nn(hi, mat) + nn(lo, mat)


def times_t(u, mat):
    hi, lo = split(u)
    return nt(hi, mat) + nt(lo, mat)


def kernel(
    points, charges, order, basis, trans, coup, top_t, top_c, out,
    pts_v, q_v, ord_v, bas_v, tr_v, cp_v, t5_v, t6_v, t7_v, t8_v, c_v,
    bs_v, uhi, ulo, side_v, lhs_v, rhs_v,
    u4_v, u4p_v, rp_v, zbuf, xbuf, u6_v, u7_v, d5_v, down_v,
    in_sem, ck_sem, cs_s, cs_r, zs, zr, xs, xr, ds_s, ds_r,
):
    me, col = lax.axis_index("leaf"), lax.axis_index("rhs")
    core = me % 2
    z = (me // 2) % NZ
    x = me // (2 * NZ)
    chip = me // 2

    def at(xx, zz, cc):
        return ((xx * NZ + zz) * 2 + cc, col)

    partner = at(x, z, 1 - core)
    zpeers = [at(x, (z + k) % NZ, core) for k in range(1, NZ)]
    xpeers = [at((x + k) % NX, z, core) for k in range(1, NX)]

    rows = CHUNK * LEAF
    order_cp = pltpu.make_async_copy(order, ord_v, in_sem.at[0])
    order_cp.start()

    def chunk_copies(c):
        return (
            pltpu.make_async_copy(basis.at[pl.ds(c * CHUNK, CHUNK)], bas_v.at[pl.ds(c * CHUNK, CHUNK)], ck_sem.at[0, c]),
            pltpu.make_async_copy(charges.at[pl.ds(c * rows, rows)], q_v.at[pl.ds(c * rows, rows)], ck_sem.at[1, c]),
        )

    for cp in chunk_copies(0):
        cp.start()
    trans_cp = pltpu.make_async_copy(trans, tr_v, in_sem.at[1])
    trans_cp.start()
    for c in range(1, LEAVES // CHUNK):
        for cp in chunk_copies(c):
            cp.start()
    late = [
        pltpu.make_async_copy(points, pts_v, in_sem.at[2]),
        pltpu.make_async_copy(coup, cp_v, in_sem.at[3]),
        pltpu.make_async_copy(top_t.at[pl.ds(x * 8, 8)], t5_v, in_sem.at[4]),
        pltpu.make_async_copy(top_t.at[pl.ds(32 + x * 4, 4)], t6_v, in_sem.at[5]),
        pltpu.make_async_copy(top_t.at[pl.ds(48 + x * 2, 2)], t7_v, in_sem.at[6]),
        pltpu.make_async_copy(top_t.at[pl.ds(56, 4)], t8_v, in_sem.at[7]),
        pltpu.make_async_copy(top_c.at[chip], c_v.at[0], in_sem.at[8]),
        pltpu.make_async_copy(top_c.at[32 + chip // 2], c_v.at[1], in_sem.at[9]),
        pltpu.make_async_copy(top_c.at[48 + chip // 4], c_v.at[2], in_sem.at[10]),
        pltpu.make_async_copy(top_c.at[56 + x], c_v.at[3], in_sem.at[11]),
        pltpu.make_async_copy(top_c.at[60 + x // 2], c_v.at[4], in_sem.at[12]),
        pltpu.make_async_copy(top_c.at[62], c_v.at[5], in_sem.at[13]),
    ]
    for cp in late:
        cp.start()

    barrier = pltpu.get_barrier_semaphore()
    peers = [partner] + zpeers + xpeers
    for peer in peers:
        pl.semaphore_signal(barrier, inc=1, device_id=peer, device_id_type=MESH)

    slot = lax.broadcasted_iota(jnp.int32, (LEAF, LEAF), 0)
    order_cp.wait()

    def put(node, u):
        hi, lo = split(u)
        uhi[node] = hi
        ulo[node] = lo
        return hi, lo

    def parent(left, right, mats):
        mats = mats.reshape(2 * RANK, RANK)
        hi = jnp.concatenate((left[0], right[0]), axis=1)
        lo = jnp.concatenate((left[1], right[1]), axis=1)
        return nn(hi, mats) + nn(lo, mats)

    def chunk(c, carry):
        for cp in chunk_copies(c):
            cp.wait()

        @pl.when(c == 0)
        def _():
            trans_cp.wait()

        ups = []
        for i in range(CHUNK):
            leaf = c * CHUNK + i
            where = ord_v[pl.ds(pl.multiple_of(leaf * LEAF, LEAF), LEAF)] & (LEAF - 1)
            pick = jnp.where(slot == where[None, :], 1.0, 0.0).astype(BF)
            own = nn(pick, bas_v[leaf]).astype(BF)
            bs_v[leaf] = own
            u = tn(q_v[pl.ds(pl.multiple_of(leaf * LEAF, LEAF), LEAF)], own)
            ups.append(put(leaf, u))
        next_ups = []
        for i in range(2):
            node = 2 * c + i
            u = parent(ups[2 * i], ups[2 * i + 1], tr_v[pl.ds(2 * node, 2)])
            next_ups.append(put(16 + node, u))
        u = parent(next_ups[0], next_ups[1], tr_v[pl.ds(16 + 2 * c, 2)])
        put(24 + c, u)
        return carry

    lax.fori_loop(0, LEAVES // CHUNK, chunk, 0)

    def read(node):
        return uhi[node], ulo[node]

    for i in range(2):
        put(28 + i, parent(read(24 + 2 * i), read(25 + 2 * i), tr_v[24 + 2 * i : 26 + 2 * i]))
    u4 = parent(read(28), read(29), tr_v[28:30])
    u4_v[...] = u4

    pl.semaphore_wait(barrier, len(peers))
    mine_rows = pl.ds(pl.multiple_of(core * HALF, HALF), HALF)
    other_rows = pl.ds(pl.multiple_of((1 - core) * HALF, HALF), HALF)

    def remote(src, dst, send, recv, peer):
        return pltpu.make_async_remote_copy(
            src_ref=src, dst_ref=dst, send_sem=send, recv_sem=recv, device_id=peer, device_id_type=MESH
        )

    swaps = [
        remote(u4_v.at[other_rows], u4p_v.at[other_rows], cs_s.at[0], cs_r.at[0], partner),
        remote(tr_v.at[30], rp_v, cs_s.at[1], cs_r.at[1], partner),
        remote(u4_v.at[mine_rows], u4p_v.at[mine_rows], cs_s.at[2], cs_r.at[2], partner),
    ]
    for cp in swaps:
        cp.start()
    for cp in late:
        cp.wait()
    swaps[0].wait_recv()
    swaps[1].wait_recv()
    u5 = times(u4_v[mine_rows], tr_v[30]) + times(u4p_v[mine_rows], rp_v[...])
    zbuf[z] = u5.astype(BF)
    zsends = [remote(zbuf.at[z], zbuf.at[z], zs.at[k], zr.at[k], zpeers[k]) for k in range(NZ - 1)]
    for k in (3, 2, 4, 1, 5, 0, 6):
        zsends[k].start()

    xs_all = pts_v[...] * SCALE
    h = xs_all.astype(BF).astype(F32)
    rest = xs_all - h
    m = rest.astype(BF).astype(F32)
    low = rest - m
    norm = jnp.sum(xs_all * xs_all, axis=0, keepdims=True)
    nh = norm.astype(BF).astype(F32)
    nrest = norm - nh
    nm = nrest.astype(BF).astype(F32)
    nl = nrest - nm
    wide = norm.shape[1]
    one = jnp.ones((1, wide), F32)
    zero = jnp.zeros((2, wide), F32)
    pad = jnp.zeros((8, wide), F32)
    lhs_v[...] = jnp.concatenate((h, h, m, m, h, low, nh, nm, nl, one, one, one, zero, pad), axis=0).astype(BF)
    rhs_v[...] = jnp.concatenate(
        (2 * h, 2 * m, 2 * h, 2 * m, 2 * low, 2 * h, -one, -one, -one, -nh, -nm, -nl, zero, pad), axis=0
    ).astype(BF)

    def direct(c, carry):
        for i in range(2):
            where = pl.ds(pl.multiple_of((2 * c + i) * LEAF, LEAF), LEAF)
            dist = tn(lhs_v[:, where], rhs_v[:, where])
            q = q_v[where]
            out[where, :] = nn(jnp.exp2(dist).astype(BF), q) + 0.5 * q.astype(F32)
        return carry

    lax.fori_loop(0, LEAVES // 2, direct, 0)

    def sides(pair, carry):
        mat = cp_v[pair]
        left, right = 2 * pair, 2 * pair + 1
        side_v[left] = nt(uhi[right], mat) + nt(ulo[right], mat)
        side_v[right] = nn(uhi[left], mat) + nn(ulo[left], mat)
        return carry

    lax.fori_loop(0, 15, sides, 0)

    swaps[2].wait_recv()

    def towards(index, bit):
        mat = c_v[index]
        return jnp.where(bit == 0, mat.astype(F32).T, mat.astype(F32)).astype(BF)

    side4 = times(u4p_v[...], towards(0, core))

    for cp in zsends:
        cp.wait_recv()
    for i in range(4):
        u6_v[i] = nn(jnp.concatenate((zbuf[2 * i], zbuf[2 * i + 1]), axis=1), t5_v[2 * i : 2 * i + 2].reshape(2 * RANK, RANK))
    for i in range(2):
        u7_v[i] = parent(split(u6_v[2 * i]), split(u6_v[2 * i + 1]), t6_v[2 * i : 2 * i + 2])
    u8 = parent(split(u7_v[0]), split(u7_v[1]), t7_v[...])
    xbuf[x] = u8.astype(BF)
    xsends = [remote(xbuf.at[x], xbuf.at[x], xs.at[k], xr.at[k], xpeers[k]) for k in range(NX - 1)]
    for k in (1, 0, 2):
        xsends[k].start()
    sib = z + 1 - 2 * (z % 2)
    side5 = nn(zbuf[sib], towards(1, z % 2))
    half_z = z // 2
    sib = half_z + 1 - 2 * (half_z % 2)
    side6 = times(u6_v[sib], towards(2, half_z % 2))
    quarter_z = z // 4
    side7 = times(u7_v[1 - quarter_z], towards(3, quarter_z))
    m8, m9 = towards(4, x % 2), towards(5, x // 2)

    for cp in xsends:
        cp.wait_recv()
    far = 2 - 2 * (x // 2)
    u9 = nn(xbuf[far], t8_v[far]) + nn(xbuf[far + 1], t8_v[far + 1])
    sib = x + 1 - 2 * (x % 2)
    d9 = times(u9, m9)
    d8 = nn(xbuf[sib], m8) + times_t(d9, t8_v[x])
    d7 = side7 + times_t(d8, t7_v[quarter_z])
    d6 = side6 + times_t(d7, t6_v[half_z])
    d5_v[mine_rows] = side5 + times_t(d6, t5_v[z])
    back = remote(d5_v.at[mine_rows], d5_v.at[mine_rows], ds_s.at[0], ds_r.at[0], partner)
    back.start()
    back.wait_recv()

    down_v[30] = side4 + times_t(d5_v[...], tr_v[30])
    for count, start in ((2, 28), (4, 24), (8, 16)):
        above = start + count
        for i in range(count):
            down_v[start + i] = side_v[start + i] + times_t(down_v[above + i // 2], tr_v[start + i])

    def final(pair, carry):
        for i in range(2):
            leaf = 2 * pair + i
            where = pl.ds(pl.multiple_of(leaf * LEAF, LEAF), LEAF)
            down = side_v[leaf] + times_t(down_v[16 + pair], tr_v[leaf])
            hi, lo = split(down)
            own = bs_v[leaf]
            out[where, :] += nt(jnp.concatenate((own, own), axis=1), jnp.concatenate((hi, lo), axis=1))
        return carry

    lax.fori_loop(0, LEAVES // 2, final, 0)

    for cp in swaps + zsends + xsends + [back]:
        cp.wait_send()


def local(*args):
    vm = pltpu.VMEM
    dma = pltpu.SemaphoreType.DMA
    rows = LEAVES * LEAF
    return pl.pallas_call(
        kernel,
        out_shape=jax.ShapeDtypeStruct((rows, COLS), F32),
        in_specs=[pl.BlockSpec(memory_space=pl.ANY)] * 8,
        out_specs=pl.BlockSpec(memory_space=pltpu.VMEM),
        scratch_shapes=[
            vm((8, rows), F32),
            vm((rows, COLS), BF),
            vm((rows,), jnp.int32),
            vm((LEAVES, LEAF, RANK), BF),
            vm((31, RANK, RANK), BF),
            vm((15, RANK, RANK), BF),
            vm((8, RANK, RANK), BF),
            vm((4, RANK, RANK), BF),
            vm((2, RANK, RANK), BF),
            vm((4, RANK, RANK), BF),
            vm((6, RANK, RANK), BF),
            vm((LEAVES, LEAF, RANK), BF),
            vm((30, COLS, RANK), BF),
            vm((30, COLS, RANK), BF),
            vm((30, COLS, RANK), F32),
            vm((64, rows), BF),
            vm((64, rows), BF),
            vm((COLS, RANK), F32),
            vm((COLS, RANK), F32),
            vm((RANK, RANK), BF),
            vm((NZ, HALF, RANK), BF),
            vm((NX, HALF, RANK), BF),
            vm((4, HALF, RANK), F32),
            vm((2, HALF, RANK), F32),
            vm((COLS, RANK), F32),
            vm((31, COLS, RANK), F32),
            dma((14,)),
            dma((2, LEAVES // CHUNK)),
            dma((3,)),
            dma((3,)),
            dma((NZ - 1,)),
            dma((NZ - 1,)),
            dma((NX - 1,)),
            dma((NX - 1,)),
            dma((1,)),
            dma((1,)),
        ],
        compiler_params=pltpu.CompilerParams(
            collective_id=0, has_side_effects=True, vmem_limit_bytes=40 * 1024 * 1024
        ),
    )(*args)


def solution(mesh):
    placed = (
        P(None, "leaf"),
        P("leaf", "rhs"),
        P("leaf"),
        P("leaf", None, None),
        P("leaf", None, None),
        P("leaf", None, None),
        P(),
        P(),
    )
    return jax.shard_map(
        local, mesh=mesh, in_specs=placed, out_specs=P("leaf", "rhs"), check_vma=False
    )
```

```python
import functools
import math

import jax
import jax.numpy as jnp
from jax import lax
from jax.experimental import pallas as pl
from jax.experimental.pallas import tpu as pltpu
from jax.sharding import PartitionSpec as P

MESH = pl.DeviceIdType.MESH
BF, F32 = jnp.bfloat16, jnp.float32
LEAF, RANK, COLS, LEAVES = 256, 128, 128, 16
HALF = COLS // 2
NZ, NX = 8, 4
SCALE = math.sqrt(0.1 * math.log2(math.e))
GROUP = 8


def nn(a, b):
    return lax.dot_general(a, b, (((1,), (0,)), ((), ())), preferred_element_type=F32)


def nt(a, b):
    return lax.dot_general(a, b, (((1,), (1,)), ((), ())), preferred_element_type=F32)


def tn(a, b):
    return lax.dot_general(a, b, (((0,), (0,)), ((), ())), preferred_element_type=F32)


def split(u):
    hi = u.astype(BF)
    return hi, (u - hi.astype(F32)).astype(BF)


def beside(*parts):
    return jnp.concatenate(parts, axis=1)


def stacked(*parts):
    return jnp.concatenate(parts, axis=0)


def times(u, mat):
    return nn(beside(*u), stacked(mat, mat))


def times_t(u, mat):
    return nt(beside(*u), beside(mat, mat))


def mat_times(mat, u):
    both = nn(mat, beside(*u))
    return both[:, :RANK] + both[:, RANK:]


def kernel(
    points, charges, order, basis, trans, coup, top_t, top_c, out,
    pts_v, q_v, ord_v, bas_v, tr_v, cp_v, t5_v, t6_v, t7_v, t8_v, c_v,
    bs_v, uhi, ulo, side_v, lhs_v, rhs_v, e_v, pick_v,
    u4_v, u4p_v, rp_v, zbuf, xbuf, d5_v, q2_v, e2_v, h_v, m_v, d2_v,
    in_sem, cs_s, cs_r, zs, zr, xs, xr, ds_s, ds_r,
):
    me, col = lax.axis_index("leaf"), lax.axis_index("rhs")
    core = me % 2
    z = (me // 2) % NZ
    x = me // (2 * NZ)
    chip = me // 2

    def at(xx, zz, cc):
        return ((xx * NZ + zz) * 2 + cc, col)

    partner = at(x, z, 1 - core)
    zpeers = [at(x, (z + k) % NZ, core) for k in range(1, NZ)]
    xpeers = [at((x + k) % NX, z, cc) for k in range(1, NX) for cc in (core, 1 - core)]

    def load(src, dst, sem):
        cp = pltpu.make_async_copy(src, dst, in_sem.at[sem])
        cp.start()
        return cp

    order_cp = load(order, ord_v, 0)
    basis_cp = load(basis, bas_v, 1)
    charges_cp = load(charges, q_v, 2)
    trans_cp = load(trans, tr_v, 3)
    late = [
        load(points, pts_v, 4),
        load(top_t.at[pl.ds(x * 8, 8)], t5_v, 5),
        load(top_t.at[pl.ds(32 + x * 4, 4)], t6_v, 6),
        load(top_t.at[pl.ds(48 + x * 2, 2)], t7_v, 7),
        load(top_t.at[pl.ds(56, 4)], t8_v, 8),
        load(top_c.at[chip], c_v.at[0], 9),
        load(top_c.at[32 + chip // 2], c_v.at[1], 10),
        load(top_c.at[48 + chip // 4], c_v.at[2], 11),
        load(top_c.at[56 + x], c_v.at[3], 12),
        load(top_c.at[60 + x // 2], c_v.at[4], 13),
        load(top_c.at[62], c_v.at[5], 14),
        load(coup, cp_v, 15),
    ]

    barrier = pltpu.get_barrier_semaphore()
    peers = [partner] + zpeers + xpeers
    for peer in peers:
        pl.semaphore_signal(barrier, inc=1, device_id=peer, device_id_type=MESH)

    def span(leaf):
        return pl.ds(leaf * LEAF, LEAF)

    slot = lax.broadcasted_iota(jnp.int32, (LEAF, LEAF), 0)
    order_cp.wait()
    for leaf in range(LEAVES):
        where = ord_v[span(leaf)] & (LEAF - 1)
        pick_v[leaf] = jnp.where(slot == where[None, :], 1.0, 0.0).astype(BF)
    basis_cp.wait()
    for leaf in range(LEAVES):
        bs_v[leaf] = nn(pick_v[leaf], bas_v[leaf]).astype(BF)
    charges_cp.wait()

    def put(node, u):
        uhi[node], ulo[node] = split(u)

    def parent(left, right, mats):
        mats = mats.reshape(2 * RANK, RANK)
        return nn(beside(left[0], right[0]), mats) + nn(beside(left[1], right[1]), mats)

    for leaf in range(LEAVES):
        put(leaf, tn(q_v[span(leaf)], bs_v[leaf]))
    trans_cp.wait()

    def read(node):
        return uhi[node], ulo[node]

    for start, count in ((0, 16), (16, 8), (24, 4)):
        for i in range(count // 2):
            low = start + 2 * i
            put(start + count + i, parent(read(low), read(low + 1), tr_v[low : low + 2]))
    u4_v[...] = parent(read(28), read(29), tr_v[28:30])

    with jax.named_scope("entry"):
        pl.semaphore_wait(barrier, len(peers))
    mine_rows = pl.ds(pl.multiple_of(core * HALF, HALF), HALF)
    other_rows = pl.ds(pl.multiple_of((1 - core) * HALF, HALF), HALF)

    def remote(src, dst, send, recv, peer):
        return pltpu.make_async_remote_copy(
            src_ref=src, dst_ref=dst, send_sem=send, recv_sem=recv, device_id=peer, device_id_type=MESH
        )

    swaps = [
        remote(u4_v.at[other_rows], u4p_v.at[other_rows], cs_s.at[0], cs_r.at[0], partner),
        remote(tr_v.at[30], rp_v, cs_s.at[1], cs_r.at[1], partner),
        remote(u4_v.at[mine_rows], u4p_v.at[mine_rows], cs_s.at[2], cs_r.at[2], partner),
    ]
    for cp in swaps:
        cp.start()
    for cp in late:
        cp.wait()

    t67 = [split(nn(t6_v[i], t7_v[i // 2])) for i in range(4)]
    for i in range(NZ):
        hi, lo = split(mat_times(t5_v[i], t67[i // 2]))
        q2_v[i * RANK : (i + 1) * RANK, :] = beside(hi, lo)
    swaps[0].wait_recv()
    swaps[1].wait_recv()
    u5 = nn(beside(*split(u4_v[mine_rows]), *split(u4p_v[mine_rows])), stacked(tr_v[30], tr_v[30], rp_v[...], rp_v[...]))
    zbuf[z] = u5.astype(BF)
    zsends = [remote(zbuf.at[z], zbuf.at[z], zs.at[k], zr.at[k], zpeers[k]) for k in range(NZ - 1)]
    for k in (3, 2, 4, 1, 5, 0, 6):
        zsends[k].start()

    xs_all = pts_v[...] * SCALE
    h = xs_all.astype(BF).astype(F32)
    rest = xs_all - h
    m = rest.astype(BF).astype(F32)
    low = rest - m
    norm = jnp.sum(xs_all * xs_all, axis=0, keepdims=True)
    nh = norm.astype(BF).astype(F32)
    nrest = norm - nh
    nm = nrest.astype(BF).astype(F32)
    nl = nrest - nm
    wide = norm.shape[1]
    one = jnp.ones((1, wide), F32)
    zero = jnp.zeros((2, wide), F32)
    pad = jnp.zeros((8, wide), F32)
    lhs_v[...] = stacked(h, h, m, m, h, low, nh, nm, nl, one, one, one, zero, pad).astype(BF)
    rhs_v[...] = stacked(2 * h, 2 * m, 2 * h, 2 * m, 2 * low, 2 * h, -one, -one, -one, -nh, -nm, -nl, zero, pad).astype(BF)

    def direct(c, carry):
        spans = [pl.ds(pl.multiple_of((GROUP * c + i) * LEAF, LEAF), LEAF) for i in range(GROUP)]
        for i, where in enumerate(spans):
            e_v[i] = jnp.exp2(tn(lhs_v[:, where], rhs_v[:, where])).astype(BF)
        for i, where in enumerate(spans):
            q = q_v[where]
            out[where, :] = nn(e_v[i], q) + 0.5 * q.astype(F32)
        return carry

    lax.fori_loop(0, LEAVES // GROUP, direct, 0)

    def towards(index, bit):
        mat = c_v[index]
        return jnp.where(bit == 0, mat.astype(F32).T, mat.astype(F32)).astype(BF)

    for i, bit in enumerate((core, z % 2, (z // 2) % 2, z // 4, x % 2, x // 2)):
        m_v[i] = towards(i, bit)

    far = 2 - 2 * (x // 2)
    rest_of_path = nn(m_v[5], t8_v[x].astype(F32).T.astype(BF))
    own_path = pl.ds(pl.multiple_of(z * RANK, RANK), RANK)
    down_path = split(mat_times(tr_v[30], (q2_v[own_path, :RANK], q2_v[own_path, RANK:])))
    from_far = split(rest_of_path)
    down_path = [split(mat_times(tr_v[28 + i], down_path)) for i in range(2)]
    across = [split(mat_times(t8_v[far + i], from_far)) for i in range(2)]
    for i in range(4):
        hi, lo = split(mat_times(tr_v[24 + i], down_path[i // 2]))
        e2_v[i * RANK : (i + 1) * RANK, :] = beside(hi, lo, hi)
    source = stacked(
        beside(m_v[4], m_v[4], jnp.zeros((RANK, RANK), BF)),
        beside(across[0][0], across[0][0], across[0][1]),
        beside(across[1][0], across[1][0], across[1][1]),
    )
    hi, lo = split(nt(source, e2_v[...]))
    h_v[: 3 * RANK] = hi
    h_v[3 * RANK :] = lo

    for pair in range(15):
        mat = cp_v[pair]
        side_v[2 * pair] = times_t(read(2 * pair + 1), mat)
        side_v[2 * pair + 1] = times(read(2 * pair), mat)

    swaps[2].wait_recv()
    side4 = times(split(u4p_v[...]), m_v[0])

    for cp in zsends:
        cp.wait_recv()
    u8 = nn(beside(*[zbuf[i] for i in range(NZ)]), q2_v[...])
    xbuf[x, mine_rows] = (u8[:, :RANK] + u8[:, RANK:]).astype(BF)
    xsends = [
        remote(xbuf.at[x, mine_rows], xbuf.at[x, mine_rows], xs.at[k], xr.at[k], xpeers[k])
        for k in range(2 * (NX - 1))
    ]
    for k in (2, 3, 0, 1, 4, 5):
        xsends[k].start()

    def sibling(i):
        return i + 1 - 2 * (i % 2)

    def level6(i):
        return split(nn(beside(zbuf[2 * i], zbuf[2 * i + 1]), stacked(t5_v[2 * i], t5_v[2 * i + 1])))

    half_z, quarter_z = z // 2, z // 4
    next6 = level6(sibling(half_z))
    other = 1 - quarter_z
    pair6 = level6(2 * other), level6(2 * other + 1)
    side5 = nn(zbuf[sibling(z)], m_v[1])
    side6 = times(next6, m_v[2])
    next7 = split(times(pair6[0], t6_v[2 * other]) + times(pair6[1], t6_v[2 * other + 1]))
    d7 = times(next7, m_v[3])
    d6 = side6 + times_t(split(d7), t6_v[half_z])
    d5_v[mine_rows] = side5 + times_t(split(d6), t5_v[z])
    back = remote(d5_v.at[mine_rows], d5_v.at[mine_rows], ds_s.at[0], ds_r.at[0], partner)
    back.start()
    back.wait_recv()
    d4 = split(side4 + times_t(split(d5_v[...]), tr_v[30]))
    d3 = [split(side_v[28 + i] + times_t(d4, tr_v[28 + i])) for i in range(2)]
    for i in range(4):
        d2_v[i] = side_v[24 + i] + times_t(d3[i // 2], tr_v[24 + i])

    for cp in xsends:
        cp.wait_recv()
    u8s = (xbuf[sibling(x)], xbuf[far], xbuf[far + 1])
    top = nn(beside(*u8s, *u8s), h_v[...])
    d2 = [split(d2_v[i] + top[:, i * RANK : (i + 1) * RANK]) for i in range(4)]
    d1 = [split(side_v[16 + i] + times_t(d2[i // 2], tr_v[16 + i])) for i in range(8)]
    for i in range(LEAVES):
        uhi[i], ulo[i] = split(side_v[i] + times_t(d1[i // 2], tr_v[i]))
    for i in range(LEAVES):
        own = bs_v[i]
        out[span(i), :] += nt(beside(own, own), beside(uhi[i], ulo[i]))

    for cp in swaps + zsends + xsends + [back]:
        cp.wait_send()


def local(*args):
    vm = pltpu.VMEM
    dma = pltpu.SemaphoreType.DMA
    rows = LEAVES * LEAF
    mats = lambda n: vm((n, RANK, RANK), BF)
    return pl.pallas_call(
        kernel,
        out_shape=jax.ShapeDtypeStruct((rows, COLS), F32),
        in_specs=[pl.BlockSpec(memory_space=pltpu.HBM)] * 8,
        out_specs=pl.BlockSpec(memory_space=pltpu.VMEM),
        scratch_shapes=[
            vm((8, rows), F32),
            vm((rows, COLS), BF),
            vm((rows,), jnp.int32),
            vm((LEAVES, LEAF, RANK), BF),
            mats(31),
            mats(15),
            mats(8),
            mats(4),
            mats(2),
            mats(4),
            mats(6),
            vm((LEAVES, LEAF, RANK), BF),
            vm((30, COLS, RANK), BF),
            vm((30, COLS, RANK), BF),
            vm((30, COLS, RANK), F32),
            vm((64, rows), BF),
            vm((64, rows), BF),
            vm((GROUP, LEAF, LEAF), BF),
            vm((LEAVES, LEAF, LEAF), BF),
            vm((COLS, RANK), F32),
            vm((COLS, RANK), F32),
            vm((RANK, RANK), BF),
            vm((NZ, HALF, RANK), BF),
            vm((NX, COLS, RANK), BF),
            vm((COLS, RANK), F32),
            vm((NZ * RANK, 2 * RANK), BF),
            vm((4 * RANK, 3 * RANK), BF),
            vm((6 * RANK, 4 * RANK), BF),
            mats(6),
            vm((4, COLS, RANK), F32),
            dma((16,)),
            dma((3,)),
            dma((3,)),
            dma((NZ - 1,)),
            dma((NZ - 1,)),
            dma((2 * (NX - 1),)),
            dma((2 * (NX - 1),)),
            dma((1,)),
            dma((1,)),
        ],
        compiler_params=pltpu.CompilerParams(
            collective_id=0, has_side_effects=True, vmem_limit_bytes=44 * 1024 * 1024
        ),
    )(*[pltpu.with_memory_space_constraint(arg, pltpu.HBM) for arg in args])


def solution(mesh):
    placed = (
        P(None, "leaf"),
        P("leaf", "rhs"),
        P("leaf"),
        P("leaf", None, None),
        P("leaf", None, None),
        P("leaf", None, None),
        P(),
        P(),
    )
    return jax.shard_map(
        local, mesh=mesh, in_specs=placed, out_specs=P("leaf", "rhs"), check_vma=False
    )
```

```python
import functools
import math

import jax
import jax.numpy as jnp
from jax import lax
from jax.experimental import pallas as pl
from jax.experimental.pallas import tpu as pltpu
from jax.sharding import PartitionSpec as P

MESH = pl.DeviceIdType.MESH
BF, F32 = jnp.bfloat16, jnp.float32
LEAF, RANK, COLS, LEAVES = 256, 128, 128, 16
HALF = COLS // 2
NZ, NX = 8, 4
SCALE = math.sqrt(0.1 * math.log2(math.e))
GROUP = 8
PARTS = 8


def nn(a, b):
    return lax.dot_general(a, b, (((1,), (0,)), ((), ())), preferred_element_type=F32)


def nt(a, b):
    return lax.dot_general(a, b, (((1,), (1,)), ((), ())), preferred_element_type=F32)


def tn(a, b):
    return lax.dot_general(a, b, (((0,), (0,)), ((), ())), preferred_element_type=F32)


def split(u):
    hi = u.astype(BF)
    return hi, (u - hi.astype(F32)).astype(BF)


def beside(*parts):
    return jnp.concatenate(parts, axis=1)


def stacked(*parts):
    return jnp.concatenate(parts, axis=0)


def times(u, mat):
    return nn(beside(*u), stacked(mat, mat))


def times_t(u, mat):
    return nt(beside(*u), beside(mat, mat))


def mat_times(mat, u):
    both = nn(mat, beside(*u))
    return both[:, :RANK] + both[:, RANK:]


def kernel(
    points, charges, order, basis, trans, coup, top_t, top_c, near, bs_v, dhi, dlo,
    pts_v, q_v, ord_v, bas_v, tr_v, cp_v, t5_v, t6_v, t7_v, t8_v, c_v,
    uhi, ulo, side_v, lhs_v, rhs_v, e_v, pick_v,
    u4_v, u4p_v, rp_v, zbuf, xbuf, d5_v, q2_v, e2_v, h_v, m_v, d2_v,
    in_sem, cs_s, cs_r, zs, zr, xs, xr, ds_s, ds_r,
):
    me, col = lax.axis_index("leaf"), lax.axis_index("rhs")
    core = me % 2
    z = (me // 2) % NZ
    x = me // (2 * NZ)
    chip = me // 2

    def at(xx, zz, cc):
        return ((xx * NZ + zz) * 2 + cc, col)

    partner = at(x, z, 1 - core)
    zpeers = [at(x, (z + k) % NZ, core) for k in range(1, NZ)]
    xpeers = [at((x + k) % NX, z, cc) for k in range(1, NX) for cc in (core, 1 - core)]

    def load(src, dst, sem):
        cp = pltpu.make_async_copy(src, dst, in_sem.at[sem])
        cp.start()
        return cp

    half = LEAVES // 2
    order_cp = load(order, ord_v, 0)
    basis_cps, charges_cps = [], []
    for i in range(2):
        part, rows = pl.ds(i * half, half), pl.ds(i * half * LEAF, half * LEAF)
        basis_cps.append(load(basis.at[part], bas_v.at[part], 1 + i))
        charges_cps.append(load(charges.at[rows], q_v.at[rows], 3 + i))
    trans_cp = load(trans, tr_v, 5)

    barrier = pltpu.get_barrier_semaphore()
    peers = [zpeers[k] for k in (3, 2, 4, 1, 5)] + xpeers + [zpeers[0], zpeers[6], partner]
    for peer in peers:
        pl.semaphore_signal(barrier, inc=1, device_id=peer, device_id_type=MESH)

    def span(leaf):
        return pl.ds(leaf * LEAF, LEAF)

    slot = lax.broadcasted_iota(jnp.int32, (LEAF, LEAF), 0)
    order_cp.wait()

    def put(node, u):
        uhi[node], ulo[node] = split(u)

    def parent(left, right, mats):
        mats = mats.reshape(2 * RANK, RANK)
        return nn(beside(left[0], right[0]), mats) + nn(beside(left[1], right[1]), mats)

    late = []
    for part in range(2):
        leaves = range(part * half, (part + 1) * half)
        for leaf in leaves:
            where = ord_v[span(leaf)] & (LEAF - 1)
            pick_v[leaf] = jnp.where(slot == where[None, :], 1.0, 0.0).astype(BF)
        basis_cps[part].wait()
        for leaf in leaves:
            bs_v[leaf] = nn(pick_v[leaf], bas_v[leaf]).astype(BF)
        charges_cps[part].wait()
        for leaf in leaves:
            put(leaf, tn(q_v[span(leaf)], bs_v[leaf]))
    trans_cp.wait()
    late = [
        load(top_t.at[pl.ds(x * 8, 8)], t5_v, 6),
        load(top_t.at[pl.ds(32 + x * 4, 4)], t6_v, 7),
        load(top_t.at[pl.ds(48 + x * 2, 2)], t7_v, 8),
        load(top_t.at[pl.ds(56, 4)], t8_v, 9),
        load(points, pts_v, 10),
        load(top_c.at[chip], c_v.at[0], 11),
        load(top_c.at[32 + chip // 2], c_v.at[1], 12),
        load(top_c.at[48 + chip // 4], c_v.at[2], 13),
        load(top_c.at[56 + x], c_v.at[3], 14),
        load(top_c.at[60 + x // 2], c_v.at[4], 15),
        load(top_c.at[62], c_v.at[5], 16),
        load(coup, cp_v, 17),
    ]

    def read(node):
        return uhi[node], ulo[node]

    for start, count in ((0, 16), (16, 8), (24, 4)):
        for i in range(count // 2):
            low = start + 2 * i
            put(start + count + i, parent(read(low), read(low + 1), tr_v[low : low + 2]))
    u4_v[...] = parent(read(28), read(29), tr_v[28:30])

    with jax.named_scope("entry"):
        pl.semaphore_wait(barrier, len(peers))
    mine_rows = pl.ds(pl.multiple_of(core * HALF, HALF), HALF)
    other_rows = pl.ds(pl.multiple_of((1 - core) * HALF, HALF), HALF)

    def remote(src, dst, send, recv, peer):
        return pltpu.make_async_remote_copy(
            src_ref=src, dst_ref=dst, send_sem=send, recv_sem=recv, device_id=peer, device_id_type=MESH
        )

    swaps = [
        remote(u4_v.at[other_rows], u4p_v.at[other_rows], cs_s.at[0], cs_r.at[0], partner),
        remote(tr_v.at[30], rp_v, cs_s.at[1], cs_r.at[1], partner),
        remote(u4_v.at[mine_rows], u4p_v.at[mine_rows], cs_s.at[2], cs_r.at[2], partner),
    ]
    for cp in swaps:
        cp.start()
    for cp in late:
        cp.wait()

    t67 = [split(nn(t6_v[i], t7_v[i // 2])) for i in range(4)]
    for i in range(NZ):
        hi, lo = split(mat_times(t5_v[i], t67[i // 2]))
        q2_v[i * RANK : (i + 1) * RANK, :] = beside(hi, lo)
    swaps[0].wait_recv()
    swaps[1].wait_recv()
    u5 = nn(beside(*split(u4_v[mine_rows]), *split(u4p_v[mine_rows])), stacked(tr_v[30], tr_v[30], rp_v[...], rp_v[...]))
    zbuf[z] = u5.astype(BF)
    zsends = [remote(zbuf.at[z], zbuf.at[z], zs.at[k], zr.at[k], zpeers[k]) for k in range(NZ - 1)]
    for k in (3, 2, 4, 1, 5, 0, 6):
        zsends[k].start()

    xs_all = pts_v[...] * SCALE
    h = xs_all.astype(BF).astype(F32)
    rest = xs_all - h
    m = rest.astype(BF).astype(F32)
    low = rest - m
    norm = jnp.sum(xs_all * xs_all, axis=0, keepdims=True)
    nh = norm.astype(BF).astype(F32)
    nrest = norm - nh
    nm = nrest.astype(BF).astype(F32)
    nl = nrest - nm
    wide = norm.shape[1]
    one = jnp.ones((1, wide), F32)
    zero = jnp.zeros((2, wide), F32)
    pad = jnp.zeros((8, wide), F32)
    lhs_v[...] = stacked(h, h, m, m, h, low, nh, nm, nl, one, one, one, zero, pad).astype(BF)
    rhs_v[...] = stacked(2 * h, 2 * m, 2 * h, 2 * m, 2 * low, 2 * h, -one, -one, -one, -nh, -nm, -nl, zero, pad).astype(BF)

    def direct(c, carry):
        spans = [pl.ds(pl.multiple_of((GROUP * c + i) * LEAF, LEAF), LEAF) for i in range(GROUP)]
        for i, where in enumerate(spans):
            e_v[i] = jnp.exp2(tn(lhs_v[:, where], rhs_v[:, where])).astype(BF)
        for i, where in enumerate(spans):
            q = q_v[where]
            near[where, :] = nn(e_v[i], q) + 0.5 * q.astype(F32)
        return carry

    lax.fori_loop(0, LEAVES // GROUP, direct, 0)

    def towards(index, bit):
        mat = c_v[index]
        return jnp.where(bit == 0, mat.astype(F32).T, mat.astype(F32)).astype(BF)

    for i, bit in enumerate((core, z % 2, (z // 2) % 2, z // 4, x % 2, x // 2)):
        m_v[i] = towards(i, bit)

    far = 2 - 2 * (x // 2)
    rest_of_path = nn(m_v[5], t8_v[x].astype(F32).T.astype(BF))
    own_path = pl.ds(pl.multiple_of(z * RANK, RANK), RANK)
    down_path = split(mat_times(tr_v[30], (q2_v[own_path, :RANK], q2_v[own_path, RANK:])))
    from_far = split(rest_of_path)
    down_path = [split(mat_times(tr_v[28 + i], down_path)) for i in range(2)]
    across = [split(mat_times(t8_v[far + i], from_far)) for i in range(2)]
    for i in range(4):
        hi, lo = split(mat_times(tr_v[24 + i], down_path[i // 2]))
        e2_v[i * RANK : (i + 1) * RANK, :] = beside(hi, lo, hi)
    source = stacked(
        beside(m_v[4], m_v[4], jnp.zeros((RANK, RANK), BF)),
        beside(across[0][0], across[0][0], across[0][1]),
        beside(across[1][0], across[1][0], across[1][1]),
    )
    hi, lo = split(nt(source, e2_v[...]))
    h_v[: 3 * RANK] = hi
    h_v[3 * RANK :] = lo

    for pair in range(15):
        mat = cp_v[pair]
        side_v[2 * pair] = times_t(read(2 * pair + 1), mat)
        side_v[2 * pair + 1] = times(read(2 * pair), mat)

    swaps[2].wait_recv()
    side4 = times(split(u4p_v[...]), m_v[0])

    for cp in zsends:
        cp.wait_recv()
    u8 = nn(beside(*[zbuf[i] for i in range(NZ)]), q2_v[...])
    xbuf[x, mine_rows] = (u8[:, :RANK] + u8[:, RANK:]).astype(BF)
    xsends = [
        remote(xbuf.at[x, mine_rows], xbuf.at[x, mine_rows], xs.at[k], xr.at[k], xpeers[k])
        for k in range(2 * (NX - 1))
    ]
    for k in (2, 3, 0, 1, 4, 5):
        xsends[k].start()

    def sibling(i):
        return i + 1 - 2 * (i % 2)

    def level6(i):
        return split(nn(beside(zbuf[2 * i], zbuf[2 * i + 1]), stacked(t5_v[2 * i], t5_v[2 * i + 1])))

    half_z, quarter_z = z // 2, z // 4
    next6 = level6(sibling(half_z))
    other = 1 - quarter_z
    pair6 = level6(2 * other), level6(2 * other + 1)
    side5 = nn(zbuf[sibling(z)], m_v[1])
    side6 = times(next6, m_v[2])
    next7 = split(times(pair6[0], t6_v[2 * other]) + times(pair6[1], t6_v[2 * other + 1]))
    d7 = times(next7, m_v[3])
    d6 = side6 + times_t(split(d7), t6_v[half_z])
    d5_v[mine_rows] = side5 + times_t(split(d6), t5_v[z])
    back = remote(d5_v.at[mine_rows], d5_v.at[mine_rows], ds_s.at[0], ds_r.at[0], partner)
    back.start()
    back.wait_recv()
    d4 = split(side4 + times_t(split(d5_v[...]), tr_v[30]))
    d3 = [split(side_v[28 + i] + times_t(d4, tr_v[28 + i])) for i in range(2)]
    for i in range(4):
        d2_v[i] = side_v[24 + i] + times_t(d3[i // 2], tr_v[24 + i])

    for cp in xsends:
        cp.wait_recv()
    u8s = (xbuf[sibling(x)], xbuf[far], xbuf[far + 1])
    top = nn(beside(*u8s, *u8s), h_v[...])
    d2 = [split(d2_v[i] + top[:, i * RANK : (i + 1) * RANK]) for i in range(4)]
    d1 = [split(side_v[16 + i] + times_t(d2[i // 2], tr_v[16 + i])) for i in range(8)]
    for i in range(LEAVES):
        dhi[i], dlo[i] = split(side_v[i] + times_t(d1[i // 2], tr_v[i]))

    for cp in swaps + zsends + xsends + [back]:
        cp.wait_send()


def finish(near, bs_v, dhi, dlo, out, sum_v, sem):
    copies = []
    for part in range(PARTS):
        count = LEAVES // PARTS
        for i in range(part * count, (part + 1) * count):
            where = pl.ds(i * LEAF, LEAF)
            own = bs_v[i]
            sum_v[where] = near[where] + nt(beside(own, own), beside(dhi[i], dlo[i]))
        where = pl.ds(part * count * LEAF, count * LEAF)
        copies.append(pltpu.make_async_copy(sum_v.at[where], out.at[where], sem.at[part]))
        copies[-1].start()
    for cp in copies:
        cp.wait()


def local(*args):
    vm = pltpu.VMEM
    dma = pltpu.SemaphoreType.DMA
    rows = LEAVES * LEAF
    mats = lambda n: vm((n, RANK, RANK), BF)
    parts = pl.pallas_call(
        kernel,
        out_shape=(vm((rows, COLS), F32), vm((LEAVES, LEAF, RANK), BF), mats(LEAVES), mats(LEAVES)),
        in_specs=[pl.BlockSpec(memory_space=pltpu.HBM)] * 8,
        out_specs=[pl.BlockSpec(memory_space=vm)] * 4,
        scratch_shapes=[
            vm((8, rows), F32),
            vm((rows, COLS), BF),
            vm((rows,), jnp.int32),
            vm((LEAVES, LEAF, RANK), BF),
            mats(31),
            mats(15),
            mats(8),
            mats(4),
            mats(2),
            mats(4),
            mats(6),
            vm((30, COLS, RANK), BF),
            vm((30, COLS, RANK), BF),
            vm((30, COLS, RANK), F32),
            vm((64, rows), BF),
            vm((64, rows), BF),
            vm((GROUP, LEAF, LEAF), BF),
            vm((LEAVES, LEAF, LEAF), BF),
            vm((COLS, RANK), F32),
            vm((COLS, RANK), F32),
            vm((RANK, RANK), BF),
            vm((NZ, HALF, RANK), BF),
            vm((NX, COLS, RANK), BF),
            vm((COLS, RANK), F32),
            vm((NZ * RANK, 2 * RANK), BF),
            vm((4 * RANK, 3 * RANK), BF),
            vm((6 * RANK, 4 * RANK), BF),
            mats(6),
            vm((4, COLS, RANK), F32),
            dma((18,)),
            dma((3,)),
            dma((3,)),
            dma((NZ - 1,)),
            dma((NZ - 1,)),
            dma((2 * (NX - 1),)),
            dma((2 * (NX - 1),)),
            dma((1,)),
            dma((1,)),
        ],
        compiler_params=pltpu.CompilerParams(
            collective_id=0, has_side_effects=True, vmem_limit_bytes=44 * 1024 * 1024
        ),
    )(*[pltpu.with_memory_space_constraint(arg, pltpu.HBM) for arg in args])
    return pl.pallas_call(
        finish,
        out_shape=jax.ShapeDtypeStruct((rows, COLS), F32),
        in_specs=[pl.BlockSpec(memory_space=vm)] * 4,
        out_specs=pl.BlockSpec(memory_space=pltpu.HBM),
        scratch_shapes=[vm((rows, COLS), F32), dma((PARTS,))],
        compiler_params=pltpu.CompilerParams(vmem_limit_bytes=16 * 1024 * 1024),
    )(*[pltpu.with_memory_space_constraint(part, vm) for part in parts])


def solution(mesh):
    placed = (
        P(None, "leaf"),
        P("leaf", "rhs"),
        P("leaf"),
        P("leaf", None, None),
        P("leaf", None, None),
        P("leaf", None, None),
        P(),
        P(),
    )
    return jax.shard_map(
        local, mesh=mesh, in_specs=placed, out_specs=P("leaf", "rhs"), check_vma=False
    )
```

```python
import functools
import math

import jax
import jax.numpy as jnp
from jax import lax
from jax.experimental import pallas as pl
from jax.experimental.pallas import tpu as pltpu
from jax.sharding import PartitionSpec as P

MESH = pl.DeviceIdType.MESH
BF, F32 = jnp.bfloat16, jnp.float32
LEAF, RANK, COLS, LEAVES = 256, 128, 128, 16
HALF = COLS // 2
NZ, NX = 8, 4
SCALE = math.sqrt(0.1 * math.log2(math.e))
GROUP = 4
PARTS = 8


def nn(a, b):
    return lax.dot_general(a, b, (((1,), (0,)), ((), ())), preferred_element_type=F32)


def nt(a, b):
    return lax.dot_general(a, b, (((1,), (1,)), ((), ())), preferred_element_type=F32)


def tn(a, b):
    return lax.dot_general(a, b, (((0,), (0,)), ((), ())), preferred_element_type=F32)


def split(u):
    hi = u.astype(BF)
    return hi, (u - hi.astype(F32)).astype(BF)


def beside(*parts):
    return jnp.concatenate(parts, axis=1)


def stacked(*parts):
    return jnp.concatenate(parts, axis=0)


def times(u, mat):
    return nn(beside(*u), stacked(mat, mat))


def times_t(u, mat):
    return nt(beside(*u), beside(mat, mat))


def mat_times(mat, u):
    both = nn(mat, beside(*u))
    return both[:, :RANK] + both[:, RANK:]


def kernel(
    points, charges, order, basis, trans, coup, top_t, top_c, near, bs_v, dhi, dlo,
    pts_v, q_v, ord_v, bas_v, tr_v, cp_v, t5_v, t6_v, t7_v, t8_v, c_v,
    uhi, ulo, side_v, lhs_v, rhs_v, e_v, pick_v,
    p_v, pp_v, u4_v, u4p_v, zbuf, xbuf, d5_v, g_v, q2_v, e0_v, src_v, h_v, m_v, d0_v,
    in_sem, cs_s, cs_r, zs, zr, xs, xr, ds_s, ds_r,
):
    me, col = lax.axis_index("leaf"), lax.axis_index("rhs")
    core = me % 2
    z = (me // 2) % NZ
    x = me // (2 * NZ)
    chip = me // 2

    def at(xx, zz, cc):
        return ((xx * NZ + zz) * 2 + cc, col)

    partner = at(x, z, 1 - core)
    zpeers = [at(x, (z + k) % NZ, core) for k in range(1, NZ)]
    xpeers = [at((x + k) % NX, z, cc) for k in range(1, NX) for cc in (core, 1 - core)]

    def load(src, dst, sem):
        cp = pltpu.make_async_copy(src, dst, in_sem.at[sem])
        cp.start()
        return cp

    order_cp = load(order, ord_v, 0)
    basis_cp = load(basis, bas_v, 1)
    charges_cp = load(charges, q_v, 2)
    trans_cp = load(trans, tr_v, 3)

    barrier = pltpu.get_barrier_semaphore()
    peers = [zpeers[k] for k in (3, 2, 4, 1, 5)] + xpeers + [zpeers[0], zpeers[6], partner]
    for peer in peers:
        pl.semaphore_signal(barrier, inc=1, device_id=peer, device_id_type=MESH)

    def span(leaf):
        return pl.ds(leaf * LEAF, LEAF)

    slot = lax.broadcasted_iota(jnp.int32, (LEAF, LEAF), 0)
    order_cp.wait()
    for leaf in range(LEAVES):
        where = ord_v[span(leaf)] & (LEAF - 1)
        pick_v[leaf] = jnp.where(slot == where[None, :], 1.0, 0.0).astype(BF)
    basis_cp.wait()
    for leaf in range(LEAVES):
        bs_v[leaf] = nn(pick_v[leaf], bas_v[leaf]).astype(BF)
    charges_cp.wait()

    def put(node, u):
        uhi[node], ulo[node] = split(u)

    def read(node):
        return uhi[node], ulo[node]

    def parent(left, right, mats):
        mats = mats.reshape(2 * RANK, RANK)
        return nn(beside(left[0], right[0]), mats) + nn(beside(left[1], right[1]), mats)

    def raise_level(start, count):
        for i in range(count // 2):
            low = start + 2 * i
            put(start + count + i, parent(read(low), read(low + 1), tr_v[low : low + 2]))

    for leaf in range(LEAVES):
        put(leaf, tn(q_v[span(leaf)], bs_v[leaf]))
    trans_cp.wait()
    late = [
        load(points, pts_v, 4),
        load(top_t.at[pl.ds(x * 8, 8)], t5_v, 5),
        load(top_t.at[pl.ds(32 + x * 4, 4)], t6_v, 6),
        load(top_t.at[pl.ds(48 + x * 2, 2)], t7_v, 7),
        load(top_t.at[pl.ds(56, 4)], t8_v, 8),
        load(top_c.at[chip], c_v.at[0], 9),
        load(top_c.at[32 + chip // 2], c_v.at[1], 10),
        load(top_c.at[48 + chip // 4], c_v.at[2], 11),
        load(top_c.at[56 + x], c_v.at[3], 12),
        load(top_c.at[60 + x // 2], c_v.at[4], 13),
        load(top_c.at[62], c_v.at[5], 14),
        load(coup, cp_v, 15),
    ]

    root = tr_v[30]
    paths = [split(nn(tr_v[28 + i], root)) for i in range(2)]
    raise_level(0, 16)
    for i in range(4):
        hi, lo = split(mat_times(tr_v[24 + i], paths[i // 2]))
        for j, part in enumerate((hi, lo, hi)):
            g_v[(4 * j + i) * RANK : (4 * j + i + 1) * RANK, :] = part
    raise_level(16, 8)
    highs = [uhi[24 + i] for i in range(4)]
    p_v[...] = nn(beside(*highs, *highs, *[ulo[24 + i] for i in range(4)]), g_v[...])

    pl.semaphore_wait(barrier, len(peers))
    mine_rows = pl.ds(pl.multiple_of(core * HALF, HALF), HALF)
    other_rows = pl.ds(pl.multiple_of((1 - core) * HALF, HALF), HALF)

    def remote(src, dst, send, recv, peer):
        return pltpu.make_async_remote_copy(
            src_ref=src, dst_ref=dst, send_sem=send, recv_sem=recv, device_id=peer, device_id_type=MESH
        )

    swap = remote(p_v.at[other_rows], pp_v, cs_s.at[0], cs_r.at[0], partner)
    swap.start()
    swap.wait_recv()
    zbuf[z] = (p_v[mine_rows] + pp_v[...]).astype(BF)
    zsends = [remote(zbuf.at[z], zbuf.at[z], zs.at[k], zr.at[k], zpeers[k]) for k in range(NZ - 1)]
    for k in (3, 2, 4, 1, 5, 0, 6):
        zsends[k].start()

    raise_level(24, 4)
    u4_v[...] = parent(read(28), read(29), tr_v[28:30])
    swap4 = remote(u4_v, u4p_v, cs_s.at[1], cs_r.at[1], partner)
    swap4.start()
    for cp in late:
        cp.wait()

    t67 = [split(nn(t6_v[i], t7_v[i // 2])) for i in range(4)]

    xs_all = pts_v[...] * SCALE
    h = xs_all.astype(BF).astype(F32)
    rest = xs_all - h
    m = rest.astype(BF).astype(F32)
    low = rest - m
    norm = jnp.sum(xs_all * xs_all, axis=0, keepdims=True)
    nh = norm.astype(BF).astype(F32)
    nrest = norm - nh
    nm = nrest.astype(BF).astype(F32)
    nl = nrest - nm
    wide = norm.shape[1]
    one = jnp.ones((1, wide), F32)
    zero = jnp.zeros((2, wide), F32)
    pad = jnp.zeros((8, wide), F32)
    lhs_v[...] = stacked(h, h, m, m, h, low, nh, nm, nl, one, one, one, zero, pad).astype(BF)
    rhs_v[...] = stacked(2 * h, 2 * m, 2 * h, 2 * m, 2 * low, 2 * h, -one, -one, -one, -nh, -nm, -nl, zero, pad).astype(BF)

    for i in range(NZ):
        hi, lo = split(mat_times(t5_v[i], t67[i // 2]))
        q2_v[i * RANK : (i + 1) * RANK, :] = beside(hi, lo)

    def towards(index, bit):
        mat = c_v[index]
        return jnp.where(bit == 0, mat.astype(F32).T, mat.astype(F32)).astype(BF)

    for i, bit in enumerate((core, z % 2, (z // 2) % 2, z // 4, x % 2, x // 2)):
        m_v[i] = towards(i, bit)

    def blocks(leaves):
        for leaf in leaves:
            where = span(leaf)
            e_v[leaf % (2 * GROUP)] = jnp.exp2(tn(lhs_v[:, where], rhs_v[:, where])).astype(BF)

    def direct(leaves):
        for leaf in leaves:
            q = q_v[span(leaf)]
            near[span(leaf), :] = nn(e_v[leaf % (2 * GROUP)], q) + 0.5 * q.astype(F32)

    far = 2 - 2 * (x // 2)
    own_path = pl.ds(pl.multiple_of(z * RANK, RANK), RANK)
    blocks(range(GROUP))
    down_path = [split(mat_times(root, (q2_v[own_path, :RANK], q2_v[own_path, RANK:])))]
    from_far = split(nn(m_v[5], t8_v[x].astype(F32).T.astype(BF)))
    across = []
    for group, start in ((0, 28), (1, 24), (2, 16), (3, 0)):
        if group < 3:
            blocks(range((group + 1) * GROUP, (group + 2) * GROUP))
        count = 2 * len(down_path)
        down_path = [split(mat_times(tr_v[start + i], down_path[i // 2])) for i in range(count)]
        if group == 0:
            across = [split(mat_times(t8_v[far + i], from_far)) for i in range(2)]
        direct(range(group * GROUP, (group + 1) * GROUP))
    for i in range(LEAVES):
        hi, lo = down_path[i]
        e0_v[i * RANK : (i + 1) * RANK, :] = beside(hi, lo, hi)
    src_v[...] = stacked(
        beside(m_v[4], m_v[4], jnp.zeros((RANK, RANK), BF)),
        beside(across[0][0], across[0][0], across[0][1]),
        beside(across[1][0], across[1][0], across[1][1]),
    )
    for pair in range(15):
        mat = cp_v[pair]
        side_v[2 * pair] = times_t(read(2 * pair + 1), mat)
        side_v[2 * pair + 1] = times(read(2 * pair), mat)

    for cp in zsends:
        cp.wait_recv()
    u8 = nn(beside(*[zbuf[i] for i in range(NZ)]), q2_v[...])
    xbuf[x, mine_rows] = (u8[:, :RANK] + u8[:, RANK:]).astype(BF)
    xsends = [
        remote(xbuf.at[x, mine_rows], xbuf.at[x, mine_rows], xs.at[k], xr.at[k], xpeers[k])
        for k in range(2 * (NX - 1))
    ]
    for k in (2, 3, 0, 1, 4, 5):
        xsends[k].start()

    def sibling(i):
        return i + 1 - 2 * (i % 2)

    def level6(i):
        return split(nn(beside(zbuf[2 * i], zbuf[2 * i + 1]), stacked(t5_v[2 * i], t5_v[2 * i + 1])))

    half_z, quarter_z = z // 2, z // 4
    other = 1 - quarter_z
    next6, pair6 = level6(sibling(half_z)), (level6(2 * other), level6(2 * other + 1))
    side5 = nn(zbuf[sibling(z)], m_v[1])
    next7 = split(times(pair6[0], t6_v[2 * other]) + times(pair6[1], t6_v[2 * other + 1]))
    side6 = times(next6, m_v[2])
    d7 = times(next7, m_v[3])
    d6 = side6 + times_t(split(d7), t6_v[half_z])
    d5_v[mine_rows] = side5 + times_t(split(d6), t5_v[z])
    back = remote(d5_v.at[mine_rows], d5_v.at[mine_rows], ds_s.at[0], ds_r.at[0], partner)
    back.start()
    for i in range(LEAVES // 2):
        where = slice(2 * i * RANK, 2 * (i + 1) * RANK)
        hi, lo = split(nt(src_v[...], e0_v[where]))
        h_v[: 3 * RANK, where] = hi
        h_v[3 * RANK :, where] = lo
    swap4.wait_recv()
    side4 = times(split(u4p_v[...]), m_v[0])
    back.wait_recv()
    down = [split(side4 + times_t(split(d5_v[...]), root))]
    for start, count in ((28, 2), (24, 4), (16, 8)):
        down = [split(side_v[start + i] + times_t(down[i // 2], tr_v[start + i])) for i in range(count)]
    for i in range(LEAVES):
        d0_v[i] = side_v[i] + times_t(down[i // 2], tr_v[i])

    for cp in xsends:
        cp.wait_recv()
    u8s = (xbuf[sibling(x)], xbuf[far], xbuf[far + 1])
    u8s = beside(*u8s, *u8s)
    for i in range(LEAVES // 2):
        top = nn(u8s, h_v[:, 2 * i * RANK : 2 * (i + 1) * RANK])
        for j in range(2):
            leaf = 2 * i + j
            dhi[leaf], dlo[leaf] = split(d0_v[leaf] + top[:, j * RANK : (j + 1) * RANK])

    for cp in [swap, swap4] + zsends + xsends + [back]:
        cp.wait_send()


def finish(near, bs_v, dhi, dlo, out, sum_v, sem):
    copies = []
    for part in range(PARTS):
        count = LEAVES // PARTS
        for i in range(part * count, (part + 1) * count):
            where = pl.ds(i * LEAF, LEAF)
            own = bs_v[i]
            sum_v[where] = near[where] + nt(beside(own, own), beside(dhi[i], dlo[i]))
        where = pl.ds(part * count * LEAF, count * LEAF)
        copies.append(pltpu.make_async_copy(sum_v.at[where], out.at[where], sem.at[part]))
        copies[-1].start()
    for cp in copies:
        cp.wait()


def local(*args):
    vm = pltpu.VMEM
    dma = pltpu.SemaphoreType.DMA
    rows = LEAVES * LEAF
    mats = lambda n: vm((n, RANK, RANK), BF)
    parts = pl.pallas_call(
        kernel,
        out_shape=(vm((rows, COLS), F32), vm((LEAVES, LEAF, RANK), BF), mats(LEAVES), mats(LEAVES)),
        in_specs=[pl.BlockSpec(memory_space=pltpu.HBM)] * 8,
        out_specs=[pl.BlockSpec(memory_space=vm)] * 4,
        scratch_shapes=[
            vm((8, rows), F32),
            vm((rows, COLS), BF),
            vm((rows,), jnp.int32),
            vm((LEAVES, LEAF, RANK), BF),
            mats(31),
            mats(15),
            mats(8),
            mats(4),
            mats(2),
            mats(4),
            mats(6),
            vm((30, COLS, RANK), BF),
            vm((30, COLS, RANK), BF),
            vm((30, COLS, RANK), F32),
            vm((64, rows), BF),
            vm((64, rows), BF),
            vm((2 * GROUP, LEAF, LEAF), BF),
            vm((LEAVES, LEAF, LEAF), BF),
            vm((COLS, RANK), F32),
            vm((HALF, RANK), F32),
            vm((COLS, RANK), F32),
            vm((COLS, RANK), F32),
            vm((NZ, HALF, RANK), BF),
            vm((NX, COLS, RANK), BF),
            vm((COLS, RANK), F32),
            vm((12 * RANK, RANK), BF),
            vm((NZ * RANK, 2 * RANK), BF),
            vm((LEAVES * RANK, 3 * RANK), BF),
            vm((3 * RANK, 3 * RANK), BF),
            vm((6 * RANK, LEAVES * RANK), BF),
            mats(6),
            vm((LEAVES, COLS, RANK), F32),
            dma((16,)),
            dma((2,)),
            dma((2,)),
            dma((NZ - 1,)),
            dma((NZ - 1,)),
            dma((2 * (NX - 1),)),
            dma((2 * (NX - 1),)),
            dma((1,)),
            dma((1,)),
        ],
        compiler_params=pltpu.CompilerParams(
            collective_id=0, has_side_effects=True, vmem_limit_bytes=44 * 1024 * 1024
        ),
    )(*[pltpu.with_memory_space_constraint(arg, pltpu.HBM) for arg in args])
    return pl.pallas_call(
        finish,
        out_shape=jax.ShapeDtypeStruct((rows, COLS), F32),
        in_specs=[pl.BlockSpec(memory_space=vm)] * 4,
        out_specs=pl.BlockSpec(memory_space=pltpu.HBM),
        scratch_shapes=[vm((rows, COLS), F32), dma((PARTS,))],
        compiler_params=pltpu.CompilerParams(vmem_limit_bytes=16 * 1024 * 1024),
    )(*[pltpu.with_memory_space_constraint(part, vm) for part in parts])


def solution(mesh):
    placed = (
        P(None, "leaf"),
        P("leaf", "rhs"),
        P("leaf"),
        P("leaf", None, None),
        P("leaf", None, None),
        P("leaf", None, None),
        P(),
        P(),
    )
    return jax.shard_map(
        local, mesh=mesh, in_specs=placed, out_specs=P("leaf", "rhs"), check_vma=False
    )
```

```python
import functools
import math

import jax
import jax.numpy as jnp
from jax import lax
from jax.experimental import pallas as pl
from jax.experimental.pallas import tpu as pltpu
from jax.sharding import PartitionSpec as P

MESH = pl.DeviceIdType.MESH
BF, F32 = jnp.bfloat16, jnp.float32
LEAF, RANK, COLS, LEAVES = 256, 128, 128, 16
HALF = COLS // 2
NZ, NX = 8, 4
SCALE = math.sqrt(0.1 * math.log2(math.e))
GROUP = 4


def nn(a, b):
    return lax.dot_general(a, b, (((1,), (0,)), ((), ())), preferred_element_type=F32)


def nt(a, b):
    return lax.dot_general(a, b, (((1,), (1,)), ((), ())), preferred_element_type=F32)


def tn(a, b):
    return lax.dot_general(a, b, (((0,), (0,)), ((), ())), preferred_element_type=F32)


def split(u):
    hi = u.astype(BF)
    return hi, (u - hi.astype(F32)).astype(BF)


def beside(*parts):
    return jnp.concatenate(parts, axis=1)


def stacked(*parts):
    return jnp.concatenate(parts, axis=0)


def times(u, mat):
    return nn(beside(*u), stacked(mat, mat))


def times_t(u, mat):
    return nt(beside(*u), beside(mat, mat))


def mat_times(mat, u):
    both = nn(mat, beside(*u))
    return both[:, :RANK] + both[:, RANK:]


def kernel(
    points, charges, order, basis, trans, coup, top_t, top_c, near, bs_v, d0_v, h_v, ups,
    pts_v, q_v, ord_v, bas_v, tr_v, cp_v, t5_v, t6_v, t7_v, t8_v, c_v,
    uhi, ulo, side_v, lhs_v, rhs_v, e_v, pick_v,
    p_v, pp_v, u4_v, u4p_v, zbuf, xbuf, d5_v, g_v, q2_v, e0_v, src_v, m_v, qp_v,
    in_sem, cs_s, cs_r, zs, zr, xs, xr, ds_s, ds_r,
):
    me, col = lax.axis_index("leaf"), lax.axis_index("rhs")
    core = me % 2
    z = (me // 2) % NZ
    x = me // (2 * NZ)
    chip = me // 2

    def at(xx, zz, cc):
        return ((xx * NZ + zz) * 2 + cc, col)

    partner = at(x, z, 1 - core)
    zpeers = [at(x, (z + k) % NZ, core) for k in range(1, NZ)]
    xpeers = [at((x + k) % NX, z, cc) for k in range(1, NX) for cc in (core, 1 - core)]

    def load(src, dst, sem):
        cp = pltpu.make_async_copy(src, dst, in_sem.at[sem])
        cp.start()
        return cp

    order_cp = load(order, ord_v, 0)
    charges_cp = load(charges, q_v, 1)
    basis_cp = load(basis, bas_v, 2)
    trans_cp = load(trans, tr_v, 3)

    barrier = pltpu.get_barrier_semaphore()
    peers = [zpeers[k] for k in (3, 2, 4, 1, 5)] + xpeers + [zpeers[0], zpeers[6], partner]
    for peer in peers:
        pl.semaphore_signal(barrier, inc=1, device_id=peer, device_id_type=MESH)

    def span(leaf):
        return pl.ds(leaf * LEAF, LEAF)

    slot = lax.broadcasted_iota(jnp.int32, (LEAF, LEAF), 0)
    order_cp.wait()
    for leaf in range(LEAVES):
        where = ord_v[span(leaf)] & (LEAF - 1)
        pick_v[leaf] = jnp.where(slot == where[None, :], 1.0, 0.0).astype(BF)
    charges_cp.wait()
    for leaf in range(LEAVES):
        qp_v[leaf] = tn(q_v[span(leaf)], pick_v[leaf]).astype(BF)
    basis_cp.wait()

    def put(node, u):
        uhi[node], ulo[node] = split(u)

    def read(node):
        return uhi[node], ulo[node]

    def parent(left, right, mats):
        mats = mats.reshape(2 * RANK, RANK)
        return nn(beside(left[0], right[0]), mats) + nn(beside(left[1], right[1]), mats)

    def raise_level(start, count):
        for i in range(count // 2):
            low = start + 2 * i
            put(start + count + i, parent(read(low), read(low + 1), tr_v[low : low + 2]))

    for leaf in range(LEAVES):
        put(leaf, nn(qp_v[leaf], bas_v[leaf]))
    trans_cp.wait()
    late = [
        load(points, pts_v, 4),
        load(top_t.at[pl.ds(x * 8, 8)], t5_v, 5),
        load(top_t.at[pl.ds(32 + x * 4, 4)], t6_v, 6),
        load(top_t.at[pl.ds(48 + x * 2, 2)], t7_v, 7),
        load(top_t.at[pl.ds(56, 4)], t8_v, 8),
        load(top_c.at[chip], c_v.at[0], 9),
        load(top_c.at[32 + chip // 2], c_v.at[1], 10),
        load(top_c.at[48 + chip // 4], c_v.at[2], 11),
        load(top_c.at[56 + x], c_v.at[3], 12),
        load(top_c.at[60 + x // 2], c_v.at[4], 13),
        load(top_c.at[62], c_v.at[5], 14),
        load(coup, cp_v, 15),
    ]

    root = tr_v[30]
    paths = [split(nn(tr_v[28 + i], root)) for i in range(2)]
    raise_level(0, 16)
    for i in range(4):
        hi, lo = split(mat_times(tr_v[24 + i], paths[i // 2]))
        for j, part in enumerate((hi, lo, hi)):
            g_v[(4 * j + i) * RANK : (4 * j + i + 1) * RANK, :] = part
    raise_level(16, 8)
    highs = [uhi[24 + i] for i in range(4)]
    p_v[...] = nn(beside(*highs, *highs, *[ulo[24 + i] for i in range(4)]), g_v[...])

    pl.semaphore_wait(barrier, len(peers))
    mine_rows = pl.ds(pl.multiple_of(core * HALF, HALF), HALF)
    other_rows = pl.ds(pl.multiple_of((1 - core) * HALF, HALF), HALF)

    def remote(src, dst, send, recv, peer):
        return pltpu.make_async_remote_copy(
            src_ref=src, dst_ref=dst, send_sem=send, recv_sem=recv, device_id=peer, device_id_type=MESH
        )

    swap = remote(p_v.at[other_rows], pp_v, cs_s.at[0], cs_r.at[0], partner)
    swap.start()
    swap.wait_recv()
    zbuf[z] = (p_v[mine_rows] + pp_v[...]).astype(BF)
    zsends = [remote(zbuf.at[z], zbuf.at[z], zs.at[k], zr.at[k], zpeers[k]) for k in range(NZ - 1)]
    for k in (3, 2, 4, 1, 5, 0, 6):
        zsends[k].start()

    raise_level(24, 4)
    u4_v[...] = parent(read(28), read(29), tr_v[28:30])
    swap4 = remote(u4_v, u4p_v, cs_s.at[1], cs_r.at[1], partner)
    swap4.start()
    for cp in late:
        cp.wait()

    t67 = [split(nn(t6_v[i], t7_v[i // 2])) for i in range(4)]

    xs_all = pts_v[...] * SCALE
    h = xs_all.astype(BF).astype(F32)
    rest = xs_all - h
    m = rest.astype(BF).astype(F32)
    low = rest - m
    norm = jnp.sum(xs_all * xs_all, axis=0, keepdims=True)
    nh = norm.astype(BF).astype(F32)
    nrest = norm - nh
    nm = nrest.astype(BF).astype(F32)
    nl = nrest - nm
    wide = norm.shape[1]
    one = jnp.ones((1, wide), F32)
    zero = jnp.zeros((2, wide), F32)
    pad = jnp.zeros((8, wide), F32)
    lhs_v[...] = stacked(h, h, m, m, h, low, nh, nm, nl, one, one, one, zero, pad).astype(BF)
    rhs_v[...] = stacked(2 * h, 2 * m, 2 * h, 2 * m, 2 * low, 2 * h, -one, -one, -one, -nh, -nm, -nl, zero, pad).astype(BF)

    for i in range(NZ):
        hi, lo = split(mat_times(t5_v[i], t67[i // 2]))
        q2_v[i * RANK : (i + 1) * RANK, :] = beside(hi, lo)

    def towards(index, bit):
        mat = c_v[index]
        return jnp.where(bit == 0, mat.astype(F32).T, mat.astype(F32)).astype(BF)

    for i, bit in enumerate((core, z % 2, (z // 2) % 2, z // 4, x % 2, x // 2)):
        m_v[i] = towards(i, bit)

    def blocks(leaves):
        for leaf in leaves:
            where = span(leaf)
            e_v[leaf % (2 * GROUP)] = jnp.exp2(tn(lhs_v[:, where], rhs_v[:, where])).astype(BF)

    def direct(leaves):
        for leaf in leaves:
            q = q_v[span(leaf)]
            near[span(leaf), :] = nn(e_v[leaf % (2 * GROUP)], q) + 0.5 * q.astype(F32)

    far = 2 - 2 * (x // 2)
    own_path = pl.ds(pl.multiple_of(z * RANK, RANK), RANK)
    blocks(range(GROUP))
    down_path = [split(mat_times(root, (q2_v[own_path, :RANK], q2_v[own_path, RANK:])))]
    from_far = split(nn(m_v[5], t8_v[x].astype(F32).T.astype(BF)))
    across = []
    for group, start in ((0, 28), (1, 24), (2, 16), (3, 0)):
        if group < 3:
            blocks(range((group + 1) * GROUP, (group + 2) * GROUP))
        count = 2 * len(down_path)
        down_path = [split(mat_times(tr_v[start + i], down_path[i // 2])) for i in range(count)]
        if group == 0:
            across = [split(mat_times(t8_v[far + i], from_far)) for i in range(2)]
        direct(range(group * GROUP, (group + 1) * GROUP))
    for i in range(LEAVES):
        hi, lo = down_path[i]
        e0_v[i * RANK : (i + 1) * RANK, :] = beside(hi, lo, hi)
    src_v[...] = stacked(
        beside(m_v[4], m_v[4], jnp.zeros((RANK, RANK), BF)),
        beside(across[0][0], across[0][0], across[0][1]),
        beside(across[1][0], across[1][0], across[1][1]),
    )
    for leaf in range(LEAVES):
        bs_v[leaf] = nn(pick_v[leaf], bas_v[leaf]).astype(BF)
    for pair in range(15):
        mat = cp_v[pair]
        side_v[2 * pair] = times_t(read(2 * pair + 1), mat)
        side_v[2 * pair + 1] = times(read(2 * pair), mat)

    for cp in zsends:
        cp.wait_recv()
    u8 = nn(beside(*[zbuf[i] for i in range(NZ)]), q2_v[...])
    xbuf[x, mine_rows] = (u8[:, :RANK] + u8[:, RANK:]).astype(BF)
    xsends = [
        remote(xbuf.at[x, mine_rows], xbuf.at[x, mine_rows], xs.at[k], xr.at[k], xpeers[k])
        for k in range(2 * (NX - 1))
    ]
    for k in (2, 3, 0, 1, 4, 5):
        xsends[k].start()

    def sibling(i):
        return i + 1 - 2 * (i % 2)

    def level6(i):
        return split(nn(beside(zbuf[2 * i], zbuf[2 * i + 1]), stacked(t5_v[2 * i], t5_v[2 * i + 1])))

    half_z, quarter_z = z // 2, z // 4
    other = 1 - quarter_z
    next6, pair6 = level6(sibling(half_z)), (level6(2 * other), level6(2 * other + 1))
    side5 = nn(zbuf[sibling(z)], m_v[1])
    next7 = split(times(pair6[0], t6_v[2 * other]) + times(pair6[1], t6_v[2 * other + 1]))
    side6 = times(next6, m_v[2])
    d7 = times(next7, m_v[3])
    d6 = side6 + times_t(split(d7), t6_v[half_z])
    d5_v[mine_rows] = side5 + times_t(split(d6), t5_v[z])
    back = remote(d5_v.at[mine_rows], d5_v.at[mine_rows], ds_s.at[0], ds_r.at[0], partner)
    back.start()
    for i in range(LEAVES // 2):
        where = slice(2 * i * RANK, 2 * (i + 1) * RANK)
        hi, lo = split(nt(src_v[...], e0_v[where]))
        h_v[: 3 * RANK, where] = hi
        h_v[3 * RANK :, where] = lo
    swap4.wait_recv()
    side4 = times(split(u4p_v[...]), m_v[0])
    back.wait_recv()
    down = [split(side4 + times_t(split(d5_v[...]), root))]
    for start, count in ((28, 2), (24, 4), (16, 8)):
        down = [split(side_v[start + i] + times_t(down[i // 2], tr_v[start + i])) for i in range(count)]
    for i in range(LEAVES):
        d0_v[i] = side_v[i] + times_t(down[i // 2], tr_v[i])

    for cp in xsends:
        cp.wait_recv()
    ups[...] = beside(xbuf[sibling(x)], xbuf[far], xbuf[far + 1])

    for cp in [swap, swap4] + zsends + xsends + [back]:
        cp.wait_send()


def finish(near, bs_v, d0_v, h_v, ups, out, sum_v, sem):
    u8s = beside(ups[...], ups[...])

    def top(i):
        return nn(u8s, h_v[:, 2 * i * RANK : 2 * (i + 1) * RANK])

    copies = []
    ahead = top(0)
    for i in range(LEAVES // 2):
        part = ahead
        if i + 1 < LEAVES // 2:
            ahead = top(i + 1)
        for j in range(2):
            leaf = 2 * i + j
            where = pl.ds(leaf * LEAF, LEAF)
            own = bs_v[leaf]
            down = split(d0_v[leaf] + part[:, j * RANK : (j + 1) * RANK])
            sum_v[where] = near[where] + nt(beside(own, own), beside(*down))
        where = pl.ds(2 * i * LEAF, 2 * LEAF)
        copies.append(pltpu.make_async_copy(sum_v.at[where], out.at[where], sem.at[i]))
        copies[-1].start()
    for cp in copies:
        cp.wait()


def local(*args):
    vm = pltpu.VMEM
    dma = pltpu.SemaphoreType.DMA
    rows = LEAVES * LEAF
    mats = lambda n: vm((n, RANK, RANK), BF)
    parts = pl.pallas_call(
        kernel,
        out_shape=(
            vm((rows, COLS), F32),
            vm((LEAVES, LEAF, RANK), BF),
            vm((LEAVES, COLS, RANK), F32),
            vm((6 * RANK, LEAVES * RANK), BF),
            vm((COLS, 3 * RANK), BF),
        ),
        in_specs=[pl.BlockSpec(memory_space=pltpu.HBM)] * 8,
        out_specs=[pl.BlockSpec(memory_space=vm)] * 5,
        scratch_shapes=[
            vm((8, rows), F32),
            vm((rows, COLS), BF),
            vm((rows,), jnp.int32),
            vm((LEAVES, LEAF, RANK), BF),
            mats(31),
            mats(15),
            mats(8),
            mats(4),
            mats(2),
            mats(4),
            mats(6),
            vm((30, COLS, RANK), BF),
            vm((30, COLS, RANK), BF),
            vm((30, COLS, RANK), F32),
            vm((64, rows), BF),
            vm((64, rows), BF),
            vm((2 * GROUP, LEAF, LEAF), BF),
            vm((LEAVES, LEAF, LEAF), BF),
            vm((COLS, RANK), F32),
            vm((HALF, RANK), F32),
            vm((COLS, RANK), F32),
            vm((COLS, RANK), F32),
            vm((NZ, HALF, RANK), BF),
            vm((NX, COLS, RANK), BF),
            vm((COLS, RANK), F32),
            vm((12 * RANK, RANK), BF),
            vm((NZ * RANK, 2 * RANK), BF),
            vm((LEAVES * RANK, 3 * RANK), BF),
            vm((3 * RANK, 3 * RANK), BF),
            mats(6),
            vm((LEAVES, COLS, LEAF), BF),
            dma((16,)),
            dma((2,)),
            dma((2,)),
            dma((NZ - 1,)),
            dma((NZ - 1,)),
            dma((2 * (NX - 1),)),
            dma((2 * (NX - 1),)),
            dma((1,)),
            dma((1,)),
        ],
        compiler_params=pltpu.CompilerParams(
            collective_id=0, has_side_effects=True, vmem_limit_bytes=44 * 1024 * 1024
        ),
    )(*[pltpu.with_memory_space_constraint(arg, pltpu.HBM) for arg in args])
    return pl.pallas_call(
        finish,
        out_shape=jax.ShapeDtypeStruct((rows, COLS), F32),
        in_specs=[pl.BlockSpec(memory_space=vm)] * 5,
        out_specs=pl.BlockSpec(memory_space=pltpu.HBM),
        scratch_shapes=[vm((rows, COLS), F32), dma((LEAVES // 2,))],
        compiler_params=pltpu.CompilerParams(vmem_limit_bytes=16 * 1024 * 1024),
    )(*[pltpu.with_memory_space_constraint(part, vm) for part in parts])


def solution(mesh):
    placed = (
        P(None, "leaf"),
        P("leaf", "rhs"),
        P("leaf"),
        P("leaf", None, None),
        P("leaf", None, None),
        P("leaf", None, None),
        P(),
        P(),
    )
    return jax.shard_map(
        local, mesh=mesh, in_specs=placed, out_specs=P("leaf", "rhs"), check_vma=False
    )
```

```python
import functools
import math

import jax
import jax.numpy as jnp
from jax import lax
from jax.experimental import pallas as pl
from jax.experimental.pallas import tpu as pltpu
from jax.sharding import PartitionSpec as P

MESH = pl.DeviceIdType.MESH
BF, F32 = jnp.bfloat16, jnp.float32
LEAF, RANK, COLS, LEAVES = 256, 128, 128, 16
HALF = COLS // 2
NZ, NX = 8, 4
SCALE = math.sqrt(0.1 * math.log2(math.e))
GROUP = 4


def nn(a, b):
    return lax.dot_general(a, b, (((1,), (0,)), ((), ())), preferred_element_type=F32)


def nt(a, b):
    return lax.dot_general(a, b, (((1,), (1,)), ((), ())), preferred_element_type=F32)


def tn(a, b):
    return lax.dot_general(a, b, (((0,), (0,)), ((), ())), preferred_element_type=F32)


def split(u):
    hi = u.astype(BF)
    return hi, (u - hi.astype(F32)).astype(BF)


def beside(*parts):
    return jnp.concatenate(parts, axis=1)


def stacked(*parts):
    return jnp.concatenate(parts, axis=0)


def times(u, mat):
    return nn(beside(*u), stacked(mat, mat))


def times_t(u, mat):
    return nt(beside(*u), beside(mat, mat))


def mat_times(mat, u):
    both = nn(mat, beside(*u))
    return both[:, :RANK] + both[:, RANK:]


def kernel(
    points, charges, order, basis, trans, coup, top_t, top_c, near, bs_v, d0_v, h_v, ups,
    pts_v, q_v, ord_v, bas_v, tr_v, cp_v, t5_v, t6_v, t7_v, t8_v, c_v,
    uhi, ulo, side_v, lhs_v, rhs_v, e_v, pick_v,
    p_v, pp_v, u4_v, u4p_v, zbuf, xbuf, d5_v, g_v, q2_v, e0_v, src_v, m_v, qp_v,
    in_sem, cs_s, cs_r, zs, zr, xs, xr, ds_s, ds_r,
):
    me, col = lax.axis_index("leaf"), lax.axis_index("rhs")
    core = me % 2
    z = (me // 2) % NZ
    x = me // (2 * NZ)
    chip = me // 2

    def at(xx, zz, cc):
        return ((xx * NZ + zz) * 2 + cc, col)

    partner = at(x, z, 1 - core)
    zpeers = [at(x, (z + k) % NZ, core) for k in range(1, NZ)]
    xpeers = [at((x + k) % NX, z, cc) for k in range(1, NX) for cc in (core, 1 - core)]

    def load(src, dst, sem):
        cp = pltpu.make_async_copy(src, dst, in_sem.at[sem])
        cp.start()
        return cp

    order_cp = load(order, ord_v, 0)
    charges_cp = load(charges, q_v, 1)
    basis_cp = load(basis, bas_v, 2)
    trans_cp = load(trans, tr_v, 3)

    barrier = pltpu.get_barrier_semaphore()
    peers = [zpeers[k] for k in (3, 2, 4, 1, 5)] + xpeers + [zpeers[0], zpeers[6], partner]
    for peer in peers:
        pl.semaphore_signal(barrier, inc=1, device_id=peer, device_id_type=MESH)

    def span(leaf):
        return pl.ds(leaf * LEAF, LEAF)

    slot = lax.broadcasted_iota(jnp.int32, (LEAF, LEAF), 0)
    order_cp.wait()
    for leaf in range(LEAVES):
        where = ord_v[span(leaf)] & (LEAF - 1)
        pick_v[leaf] = jnp.where(slot == where[None, :], 1.0, 0.0).astype(BF)
    charges_cp.wait()
    for leaf in range(LEAVES):
        qp_v[leaf] = tn(q_v[span(leaf)], pick_v[leaf]).astype(BF)
    basis_cp.wait()

    def put(node, u):
        uhi[node], ulo[node] = split(u)

    def read(node):
        return uhi[node], ulo[node]

    def parent(left, right, mats):
        mats = mats.reshape(2 * RANK, RANK)
        return nn(beside(left[0], right[0]), mats) + nn(beside(left[1], right[1]), mats)

    def raise_level(start, count):
        for i in range(count // 2):
            low = start + 2 * i
            put(start + count + i, parent(read(low), read(low + 1), tr_v[low : low + 2]))

    for leaf in range(LEAVES):
        put(leaf, nn(qp_v[leaf], bas_v[leaf]))
    trans_cp.wait()

    root = tr_v[30]
    paths = [split(nn(tr_v[28 + i], root)) for i in range(2)]
    raise_level(0, 16)
    for i in range(4):
        hi, lo = split(mat_times(tr_v[24 + i], paths[i // 2]))
        for j, part in enumerate((hi, lo, hi)):
            g_v[(4 * j + i) * RANK : (4 * j + i + 1) * RANK, :] = part
    raise_level(16, 8)
    highs = [uhi[24 + i] for i in range(4)]
    p_v[...] = nn(beside(*highs, *highs, *[ulo[24 + i] for i in range(4)]), g_v[...])

    pl.semaphore_wait(barrier, len(peers))
    mine_rows = pl.ds(pl.multiple_of(core * HALF, HALF), HALF)
    other_rows = pl.ds(pl.multiple_of((1 - core) * HALF, HALF), HALF)

    def remote(src, dst, send, recv, peer):
        return pltpu.make_async_remote_copy(
            src_ref=src, dst_ref=dst, send_sem=send, recv_sem=recv, device_id=peer, device_id_type=MESH
        )

    swap = remote(p_v.at[other_rows], pp_v, cs_s.at[0], cs_r.at[0], partner)
    swap.start()
    late = [
        load(points, pts_v, 4),
        load(top_t.at[pl.ds(x * 8, 8)], t5_v, 5),
        load(top_t.at[pl.ds(32 + x * 4, 4)], t6_v, 6),
        load(top_t.at[pl.ds(48 + x * 2, 2)], t7_v, 7),
        load(top_t.at[pl.ds(56, 4)], t8_v, 8),
        load(top_c.at[chip], c_v.at[0], 9),
        load(top_c.at[32 + chip // 2], c_v.at[1], 10),
        load(top_c.at[48 + chip // 4], c_v.at[2], 11),
        load(top_c.at[56 + x], c_v.at[3], 12),
        load(top_c.at[60 + x // 2], c_v.at[4], 13),
        load(top_c.at[62], c_v.at[5], 14),
        load(coup, cp_v, 15),
    ]
    swap.wait_recv()
    zbuf[z] = (p_v[mine_rows] + pp_v[...]).astype(BF)
    zsends = [remote(zbuf.at[z], zbuf.at[z], zs.at[k], zr.at[k], zpeers[k]) for k in range(NZ - 1)]
    for k in (3, 2, 4, 1, 5, 0, 6):
        zsends[k].start()

    raise_level(24, 4)
    u4_v[...] = parent(read(28), read(29), tr_v[28:30])
    swap4 = remote(u4_v, u4p_v, cs_s.at[1], cs_r.at[1], partner)
    swap4.start()
    for cp in late:
        cp.wait()

    t67 = [split(nn(t6_v[i], t7_v[i // 2])) for i in range(4)]

    xs_all = pts_v[...] * SCALE
    h = xs_all.astype(BF).astype(F32)
    rest = xs_all - h
    m = rest.astype(BF).astype(F32)
    low = rest - m
    norm = jnp.sum(xs_all * xs_all, axis=0, keepdims=True)
    nh = norm.astype(BF).astype(F32)
    nrest = norm - nh
    nm = nrest.astype(BF).astype(F32)
    nl = nrest - nm
    wide = norm.shape[1]
    one = jnp.ones((1, wide), F32)
    zero = jnp.zeros((2, wide), F32)
    pad = jnp.zeros((8, wide), F32)
    lhs_v[...] = stacked(h, h, m, m, h, low, nh, nm, nl, one, one, one, zero, pad).astype(BF)
    rhs_v[...] = stacked(2 * h, 2 * m, 2 * h, 2 * m, 2 * low, 2 * h, -one, -one, -one, -nh, -nm, -nl, zero, pad).astype(BF)

    for i in range(NZ):
        hi, lo = split(mat_times(t5_v[i], t67[i // 2]))
        q2_v[i * RANK : (i + 1) * RANK, :] = beside(hi, lo)

    def towards(index, bit):
        mat = c_v[index]
        return jnp.where(bit == 0, mat.astype(F32).T, mat.astype(F32)).astype(BF)

    for i, bit in enumerate((core, z % 2, (z // 2) % 2, z // 4, x % 2, x // 2)):
        m_v[i] = towards(i, bit)

    def blocks(leaves):
        for leaf in leaves:
            where = span(leaf)
            e_v[leaf % (2 * GROUP)] = jnp.exp2(tn(lhs_v[:, where], rhs_v[:, where])).astype(BF)

    def direct(leaves):
        for leaf in leaves:
            q = q_v[span(leaf)]
            near[span(leaf), :] = nn(e_v[leaf % (2 * GROUP)], q) + 0.5 * q.astype(F32)

    far = 2 - 2 * (x // 2)
    own_path = pl.ds(pl.multiple_of(z * RANK, RANK), RANK)
    blocks(range(GROUP))
    down_path = [split(mat_times(root, (q2_v[own_path, :RANK], q2_v[own_path, RANK:])))]
    from_far = split(nn(m_v[5], t8_v[x].astype(F32).T.astype(BF)))
    across = []
    for group, start in ((0, 28), (1, 24), (2, 16), (3, 0)):
        if group < 3:
            blocks(range((group + 1) * GROUP, (group + 2) * GROUP))
        count = 2 * len(down_path)
        down_path = [split(mat_times(tr_v[start + i], down_path[i // 2])) for i in range(count)]
        if group == 0:
            across = [split(mat_times(t8_v[far + i], from_far)) for i in range(2)]
        direct(range(group * GROUP, (group + 1) * GROUP))
    for i in range(LEAVES):
        hi, lo = down_path[i]
        e0_v[i * RANK : (i + 1) * RANK, :] = beside(hi, lo, hi)
    src_v[...] = stacked(
        beside(m_v[4], m_v[4], jnp.zeros((RANK, RANK), BF)),
        beside(across[0][0], across[0][0], across[0][1]),
        beside(across[1][0], across[1][0], across[1][1]),
    )
    for leaf in range(LEAVES):
        bs_v[leaf] = nn(pick_v[leaf], bas_v[leaf]).astype(BF)
    for pair in range(15):
        mat = cp_v[pair]
        side_v[2 * pair] = times_t(read(2 * pair + 1), mat)
        side_v[2 * pair + 1] = times(read(2 * pair), mat)

    for cp in zsends:
        cp.wait_recv()
    u8 = nn(beside(*[zbuf[i] for i in range(NZ)]), q2_v[...])
    xbuf[x, mine_rows] = (u8[:, :RANK] + u8[:, RANK:]).astype(BF)
    xsends = [
        remote(xbuf.at[x, mine_rows], xbuf.at[x, mine_rows], xs.at[k], xr.at[k], xpeers[k])
        for k in range(2 * (NX - 1))
    ]
    for k in (2, 3, 0, 1, 4, 5):
        xsends[k].start()

    def sibling(i):
        return i + 1 - 2 * (i % 2)

    def level6(i):
        return split(nn(beside(zbuf[2 * i], zbuf[2 * i + 1]), stacked(t5_v[2 * i], t5_v[2 * i + 1])))

    half_z, quarter_z = z // 2, z // 4
    other = 1 - quarter_z
    next6, pair6 = level6(sibling(half_z)), (level6(2 * other), level6(2 * other + 1))
    side5 = nn(zbuf[sibling(z)], m_v[1])
    next7 = split(times(pair6[0], t6_v[2 * other]) + times(pair6[1], t6_v[2 * other + 1]))
    side6 = times(next6, m_v[2])
    d7 = times(next7, m_v[3])
    d6 = side6 + times_t(split(d7), t6_v[half_z])
    d5_v[mine_rows] = side5 + times_t(split(d6), t5_v[z])
    back = remote(d5_v.at[mine_rows], d5_v.at[mine_rows], ds_s.at[0], ds_r.at[0], partner)
    back.start()
    for i in range(LEAVES // 2):
        where = slice(2 * i * RANK, 2 * (i + 1) * RANK)
        hi, lo = split(nt(src_v[...], e0_v[where]))
        h_v[: 3 * RANK, where] = hi
        h_v[3 * RANK :, where] = lo
    swap4.wait_recv()
    side4 = times(split(u4p_v[...]), m_v[0])
    back.wait_recv()
    down = [split(side4 + times_t(split(d5_v[...]), root))]
    for start, count in ((28, 2), (24, 4), (16, 8)):
        down = [split(side_v[start + i] + times_t(down[i // 2], tr_v[start + i])) for i in range(count)]
    for i in range(LEAVES):
        d0_v[i] = side_v[i] + times_t(down[i // 2], tr_v[i])

    for cp in xsends:
        cp.wait_recv()
    ups[...] = beside(xbuf[sibling(x)], xbuf[far], xbuf[far + 1])

    for cp in [swap, swap4] + zsends + xsends + [back]:
        cp.wait_send()


def finish(near, bs_v, d0_v, h_v, ups, out, sum_v, sem):
    u8s = beside(ups[...], ups[...])
    pairs = LEAVES // 2
    tops, downs, copies = {}, {}, []

    def final(i):
        for leaf in (2 * i, 2 * i + 1):
            where = pl.ds(leaf * LEAF, LEAF)
            own = bs_v[leaf]
            sum_v[where] = near[where] + nt(beside(own, own), beside(*downs[leaf]))
        where = pl.ds(2 * i * LEAF, 2 * LEAF)
        copies.append(pltpu.make_async_copy(sum_v.at[where], out.at[where], sem.at[i]))
        copies[-1].start()

    for step in range(pairs + 2):
        if step < pairs:
            tops[step] = nn(u8s, h_v[:, 2 * step * RANK : 2 * (step + 1) * RANK])
        if 1 <= step <= pairs:
            for j in range(2):
                leaf = 2 * (step - 1) + j
                downs[leaf] = split(d0_v[leaf] + tops[step - 1][:, j * RANK : (j + 1) * RANK])
        if step >= 2:
            final(step - 2)
    for cp in copies:
        cp.wait()


def local(*args):
    vm = pltpu.VMEM
    dma = pltpu.SemaphoreType.DMA
    rows = LEAVES * LEAF
    mats = lambda n: vm((n, RANK, RANK), BF)
    parts = pl.pallas_call(
        kernel,
        out_shape=(
            vm((rows, COLS), F32),
            vm((LEAVES, LEAF, RANK), BF),
            vm((LEAVES, COLS, RANK), F32),
            vm((6 * RANK, LEAVES * RANK), BF),
            vm((COLS, 3 * RANK), BF),
        ),
        in_specs=[pl.BlockSpec(memory_space=pltpu.HBM)] * 8,
        out_specs=[pl.BlockSpec(memory_space=vm)] * 5,
        scratch_shapes=[
            vm((8, rows), F32),
            vm((rows, COLS), BF),
            vm((rows,), jnp.int32),
            vm((LEAVES, LEAF, RANK), BF),
            mats(31),
            mats(15),
            mats(8),
            mats(4),
            mats(2),
            mats(4),
            mats(6),
            vm((30, COLS, RANK), BF),
            vm((30, COLS, RANK), BF),
            vm((30, COLS, RANK), F32),
            vm((64, rows), BF),
            vm((64, rows), BF),
            vm((2 * GROUP, LEAF, LEAF), BF),
            vm((LEAVES, LEAF, LEAF), BF),
            vm((COLS, RANK), F32),
            vm((HALF, RANK), F32),
            vm((COLS, RANK), F32),
            vm((COLS, RANK), F32),
            vm((NZ, HALF, RANK), BF),
            vm((NX, COLS, RANK), BF),
            vm((COLS, RANK), F32),
            vm((12 * RANK, RANK), BF),
            vm((NZ * RANK, 2 * RANK), BF),
            vm((LEAVES * RANK, 3 * RANK), BF),
            vm((3 * RANK, 3 * RANK), BF),
            mats(6),
            vm((LEAVES, COLS, LEAF), BF),
            dma((16,)),
            dma((2,)),
            dma((2,)),
            dma((NZ - 1,)),
            dma((NZ - 1,)),
            dma((2 * (NX - 1),)),
            dma((2 * (NX - 1),)),
            dma((1,)),
            dma((1,)),
        ],
        compiler_params=pltpu.CompilerParams(
            collective_id=0, has_side_effects=True, vmem_limit_bytes=44 * 1024 * 1024
        ),
    )(*[pltpu.with_memory_space_constraint(arg, pltpu.HBM) for arg in args])
    return pl.pallas_call(
        finish,
        out_shape=jax.ShapeDtypeStruct((rows, COLS), F32),
        in_specs=[pl.BlockSpec(memory_space=vm)] * 5,
        out_specs=pl.BlockSpec(memory_space=pltpu.HBM),
        scratch_shapes=[vm((rows, COLS), F32), dma((LEAVES // 2,))],
        compiler_params=pltpu.CompilerParams(vmem_limit_bytes=16 * 1024 * 1024),
    )(*[pltpu.with_memory_space_constraint(part, vm) for part in parts])


def solution(mesh):
    placed = (
        P(None, "leaf"),
        P("leaf", "rhs"),
        P("leaf"),
        P("leaf", None, None),
        P("leaf", None, None),
        P("leaf", None, None),
        P(),
        P(),
    )
    return jax.shard_map(
        local, mesh=mesh, in_specs=placed, out_specs=P("leaf", "rhs"), check_vma=False
    )
```

```python
import functools
import math

import jax
import jax.numpy as jnp
from jax import lax
from jax.experimental import pallas as pl
from jax.experimental.pallas import tpu as pltpu
from jax.sharding import PartitionSpec as P

MESH = pl.DeviceIdType.MESH
BF, F32 = jnp.bfloat16, jnp.float32
LEAF, RANK, COLS, LEAVES = 256, 128, 128, 16
HALF = COLS // 2
NZ, NX = 8, 4
SCALE = math.sqrt(0.1 * math.log2(math.e))
GROUP = 4


def nn(a, b):
    return lax.dot_general(a, b, (((1,), (0,)), ((), ())), preferred_element_type=F32)


def nt(a, b):
    return lax.dot_general(a, b, (((1,), (1,)), ((), ())), preferred_element_type=F32)


def tn(a, b):
    return lax.dot_general(a, b, (((0,), (0,)), ((), ())), preferred_element_type=F32)


def split(u):
    hi = u.astype(BF)
    return hi, (u - hi.astype(F32)).astype(BF)


def beside(*parts):
    return jnp.concatenate(parts, axis=1)


def stacked(*parts):
    return jnp.concatenate(parts, axis=0)


def times(u, mat):
    return nn(beside(*u), stacked(mat, mat))


def times_t(u, mat):
    return nt(beside(*u), beside(mat, mat))


def mat_times(mat, u):
    both = nn(mat, beside(*u))
    return both[:, :RANK] + both[:, RANK:]


def kernel(
    points, charges, order, basis, trans, coup, top_t, top_c, near, bs_v, d0_v, h_v, ups,
    pts_v, q_v, ord_v, bas_v, tr_v, cp_v, t5_v, t6_v, t7_v, t8_v, c_v,
    uhi, ulo, side_v, lhs_v, rhs_v, e_v, pick_v,
    p_v, pp_v, u4_v, u4p_v, zbuf, xbuf, d5_v, g_v, q2_v, e0_v, src_v, m_v, qp_v,
    in_sem, cs_s, cs_r, zs, zr, xs, xr, ds_s, ds_r,
):
    me, col = lax.axis_index("leaf"), lax.axis_index("rhs")
    core = me % 2
    z = (me // 2) % NZ
    x = me // (2 * NZ)
    chip = me // 2

    def at(xx, zz, cc):
        return ((xx * NZ + zz) * 2 + cc, col)

    partner = at(x, z, 1 - core)
    zpeers = [at(x, (z + k) % NZ, core) for k in range(1, NZ)]
    xpeers = [at((x + k) % NX, z, cc) for k in range(1, NX) for cc in (core, 1 - core)]

    def load(src, dst, sem):
        cp = pltpu.make_async_copy(src, dst, in_sem.at[sem])
        cp.start()
        return cp

    barrier = pltpu.get_barrier_semaphore()
    peers = [zpeers[k] for k in (3, 2, 4, 1, 5)] + xpeers + [zpeers[0], zpeers[6], partner]
    for peer in peers[:5]:
        pl.semaphore_signal(barrier, inc=1, device_id=peer, device_id_type=MESH)

    order_cp = load(order, ord_v, 0)
    charges_cp = load(charges, q_v, 1)
    basis_cp = load(basis, bas_v, 2)
    trans_cp = load(trans, tr_v, 3)
    for peer in peers[5:]:
        pl.semaphore_signal(barrier, inc=1, device_id=peer, device_id_type=MESH)

    def span(leaf):
        return pl.ds(leaf * LEAF, LEAF)

    slot = lax.broadcasted_iota(jnp.int32, (LEAF, LEAF), 0)
    order_cp.wait()
    for leaf in range(LEAVES):
        where = ord_v[span(leaf)] & (LEAF - 1)
        pick_v[leaf] = jnp.where(slot == where[None, :], 1.0, 0.0).astype(BF)
    charges_cp.wait()
    for leaf in range(LEAVES):
        qp_v[leaf] = tn(q_v[span(leaf)], pick_v[leaf]).astype(BF)
    basis_cp.wait()

    def put(node, u):
        uhi[node], ulo[node] = split(u)

    def read(node):
        return uhi[node], ulo[node]

    def parent(left, right, mats):
        mats = mats.reshape(2 * RANK, RANK)
        return nn(beside(left[0], right[0]), mats) + nn(beside(left[1], right[1]), mats)

    def raise_level(start, count):
        for i in range(count // 2):
            low = start + 2 * i
            put(start + count + i, parent(read(low), read(low + 1), tr_v[low : low + 2]))

    for leaf in range(LEAVES):
        put(leaf, nn(qp_v[leaf], bas_v[leaf]))
    trans_cp.wait()

    root = tr_v[30]
    paths = [split(nn(tr_v[28 + i], root)) for i in range(2)]
    raise_level(0, 16)
    for i in range(4):
        hi, lo = split(mat_times(tr_v[24 + i], paths[i // 2]))
        g_v[i * RANK : (i + 1) * RANK, :] = beside(hi, lo)
    raise_level(16, 8)
    both = nn(beside(*[uhi[24 + i] for i in range(4)]), g_v[...])
    p_v[...] = both[:, :RANK] + both[:, RANK:] + nn(beside(*[ulo[24 + i] for i in range(4)]), g_v[:, :RANK])

    pl.semaphore_wait(barrier, len(peers))
    mine_rows = pl.ds(pl.multiple_of(core * HALF, HALF), HALF)
    other_rows = pl.ds(pl.multiple_of((1 - core) * HALF, HALF), HALF)

    def remote(src, dst, send, recv, peer):
        return pltpu.make_async_remote_copy(
            src_ref=src, dst_ref=dst, send_sem=send, recv_sem=recv, device_id=peer, device_id_type=MESH
        )

    swap = remote(p_v.at[other_rows], pp_v, cs_s.at[0], cs_r.at[0], partner)
    swap.start()
    late = [
        load(points, pts_v, 4),
        load(top_t.at[pl.ds(x * 8, 8)], t5_v, 5),
        load(top_t.at[pl.ds(32 + x * 4, 4)], t6_v, 6),
        load(top_t.at[pl.ds(48 + x * 2, 2)], t7_v, 7),
        load(top_t.at[pl.ds(56, 4)], t8_v, 8),
        load(top_c.at[chip], c_v.at[0], 9),
        load(top_c.at[32 + chip // 2], c_v.at[1], 10),
        load(top_c.at[48 + chip // 4], c_v.at[2], 11),
        load(top_c.at[56 + x], c_v.at[3], 12),
        load(top_c.at[60 + x // 2], c_v.at[4], 13),
        load(top_c.at[62], c_v.at[5], 14),
        load(coup, cp_v, 15),
    ]
    swap.wait_recv()
    zbuf[z] = (p_v[mine_rows] + pp_v[...]).astype(BF)
    zsends = [remote(zbuf.at[z], zbuf.at[z], zs.at[k], zr.at[k], zpeers[k]) for k in range(NZ - 1)]
    for k in (3, 4, 2, 5, 1, 6, 0):
        zsends[k].start()

    raise_level(24, 4)
    u4_v[...] = parent(read(28), read(29), tr_v[28:30])
    swap4 = remote(u4_v, u4p_v, cs_s.at[1], cs_r.at[1], partner)
    swap4.start()
    for cp in late:
        cp.wait()

    t67 = [split(nn(t6_v[i], t7_v[i // 2])) for i in range(4)]

    xs_all = pts_v[...] * SCALE
    h = xs_all.astype(BF).astype(F32)
    rest = xs_all - h
    m = rest.astype(BF).astype(F32)
    low = rest - m
    norm = jnp.sum(xs_all * xs_all, axis=0, keepdims=True)
    nh = norm.astype(BF).astype(F32)
    nrest = norm - nh
    nm = nrest.astype(BF).astype(F32)
    nl = nrest - nm
    wide = norm.shape[1]
    one = jnp.ones((1, wide), F32)
    zero = jnp.zeros((2, wide), F32)
    pad = jnp.zeros((8, wide), F32)
    lhs_v[...] = stacked(h, h, m, m, h, low, nh, nm, nl, one, one, one, zero, pad).astype(BF)
    rhs_v[...] = stacked(2 * h, 2 * m, 2 * h, 2 * m, 2 * low, 2 * h, -one, -one, -one, -nh, -nm, -nl, zero, pad).astype(BF)

    for i in range(NZ):
        hi, lo = split(mat_times(t5_v[i], t67[i // 2]))
        q2_v[i * RANK : (i + 1) * RANK, :] = beside(hi, lo)

    def towards(index, bit):
        mat = c_v[index]
        return jnp.where(bit == 0, mat.astype(F32).T, mat.astype(F32)).astype(BF)

    for i, bit in enumerate((core, z % 2, (z // 2) % 2, z // 4, x % 2, x // 2)):
        m_v[i] = towards(i, bit)

    def blocks(leaves):
        for leaf in leaves:
            where = span(leaf)
            e_v[leaf % (2 * GROUP)] = jnp.exp2(tn(lhs_v[:, where], rhs_v[:, where])).astype(BF)

    def direct(leaves):
        for leaf in leaves:
            q = q_v[span(leaf)]
            near[span(leaf), :] = nn(e_v[leaf % (2 * GROUP)], q) + 0.5 * q.astype(F32)

    far = 2 - 2 * (x // 2)
    own_path = pl.ds(pl.multiple_of(z * RANK, RANK), RANK)
    blocks(range(GROUP))
    down_path = [split(mat_times(root, (q2_v[own_path, :RANK], q2_v[own_path, RANK:])))]
    from_far = split(nn(m_v[5], t8_v[x].astype(F32).T.astype(BF)))
    across = []
    for group, start in ((0, 28), (1, 24), (2, 16), (3, 0)):
        if group < 3:
            blocks(range((group + 1) * GROUP, (group + 2) * GROUP))
        count = 2 * len(down_path)
        down_path = [split(mat_times(tr_v[start + i], down_path[i // 2])) for i in range(count)]
        if group == 0:
            across = [split(mat_times(t8_v[far + i], from_far)) for i in range(2)]
        direct(range(group * GROUP, (group + 1) * GROUP))
    for i in range(LEAVES):
        hi, lo = down_path[i]
        e0_v[i * RANK : (i + 1) * RANK, :] = beside(hi, lo, hi)
    src_v[...] = stacked(
        beside(m_v[4], m_v[4], jnp.zeros((RANK, RANK), BF)),
        beside(across[0][0], across[0][0], across[0][1]),
        beside(across[1][0], across[1][0], across[1][1]),
    )
    for leaf in range(LEAVES):
        bs_v[leaf] = nn(pick_v[leaf], bas_v[leaf]).astype(BF)
    for pair in range(15):
        mat = cp_v[pair]
        side_v[2 * pair] = times_t(read(2 * pair + 1), mat)
        side_v[2 * pair + 1] = times(read(2 * pair), mat)

    for cp in zsends:
        cp.wait_recv()
    u8 = nn(beside(*[zbuf[i] for i in range(NZ)]), q2_v[...])
    xbuf[x, mine_rows] = (u8[:, :RANK] + u8[:, RANK:]).astype(BF)
    xsends = [
        remote(xbuf.at[x, mine_rows], xbuf.at[x, mine_rows], xs.at[k], xr.at[k], xpeers[k])
        for k in range(2 * (NX - 1))
    ]
    for k in (2, 3, 0, 1, 4, 5):
        xsends[k].start()

    def sibling(i):
        return i + 1 - 2 * (i % 2)

    def level6(i):
        return split(nn(beside(zbuf[2 * i], zbuf[2 * i + 1]), stacked(t5_v[2 * i], t5_v[2 * i + 1])))

    half_z, quarter_z = z // 2, z // 4
    other = 1 - quarter_z
    next6, pair6 = level6(sibling(half_z)), (level6(2 * other), level6(2 * other + 1))
    side5 = nn(zbuf[sibling(z)], m_v[1])
    next7 = split(times(pair6[0], t6_v[2 * other]) + times(pair6[1], t6_v[2 * other + 1]))
    side6 = times(next6, m_v[2])
    d7 = times(next7, m_v[3])
    d6 = side6 + times_t(split(d7), t6_v[half_z])
    d5_v[mine_rows] = side5 + times_t(split(d6), t5_v[z])
    back = remote(d5_v.at[mine_rows], d5_v.at[mine_rows], ds_s.at[0], ds_r.at[0], partner)
    back.start()
    for i in range(LEAVES // 2):
        where = slice(2 * i * RANK, 2 * (i + 1) * RANK)
        hi, lo = split(nt(src_v[...], e0_v[where]))
        h_v[: 3 * RANK, where] = hi
        h_v[3 * RANK :, where] = lo
    swap4.wait_recv()
    side4 = times(split(u4p_v[...]), m_v[0])
    back.wait_recv()
    down = [split(side4 + times_t(split(d5_v[...]), root))]
    for start, count in ((28, 2), (24, 4), (16, 8)):
        down = [split(side_v[start + i] + times_t(down[i // 2], tr_v[start + i])) for i in range(count)]
    for i in range(LEAVES):
        d0_v[i] = side_v[i] + times_t(down[i // 2], tr_v[i])

    for cp in [swap, swap4, back] + zsends + xsends:
        cp.wait_send()
    for cp in xsends:
        cp.wait_recv()
    ups[...] = beside(xbuf[sibling(x)], xbuf[far], xbuf[far + 1])


def finish(near, bs_v, d0_v, h_v, ups, out, sum_v, sem):
    u8s = beside(ups[...], ups[...])
    pairs = LEAVES // 2
    tops, downs, copies = {}, {}, []

    def final(i):
        for leaf in (2 * i, 2 * i + 1):
            where = pl.ds(leaf * LEAF, LEAF)
            own = bs_v[leaf]
            sum_v[where] = near[where] + nt(beside(own, own), beside(*downs[leaf]))
        where = pl.ds(2 * i * LEAF, 2 * LEAF)
        copies.append(pltpu.make_async_copy(sum_v.at[where], out.at[where], sem.at[i]))
        copies[-1].start()

    for step in range(pairs + 2):
        if step < pairs:
            tops[step] = nn(u8s, h_v[:, 2 * step * RANK : 2 * (step + 1) * RANK])
        if 1 <= step <= pairs:
            for j in range(2):
                leaf = 2 * (step - 1) + j
                downs[leaf] = split(d0_v[leaf] + tops[step - 1][:, j * RANK : (j + 1) * RANK])
        if step >= 2:
            final(step - 2)
    for cp in copies:
        cp.wait()


def local(*args):
    vm = pltpu.VMEM
    dma = pltpu.SemaphoreType.DMA
    rows = LEAVES * LEAF
    mats = lambda n: vm((n, RANK, RANK), BF)
    parts = pl.pallas_call(
        kernel,
        out_shape=(
            vm((rows, COLS), F32),
            vm((LEAVES, LEAF, RANK), BF),
            vm((LEAVES, COLS, RANK), F32),
            vm((6 * RANK, LEAVES * RANK), BF),
            vm((COLS, 3 * RANK), BF),
        ),
        in_specs=[pl.BlockSpec(memory_space=pltpu.HBM)] * 8,
        out_specs=[pl.BlockSpec(memory_space=vm)] * 5,
        scratch_shapes=[
            vm((8, rows), F32),
            vm((rows, COLS), BF),
            vm((rows,), jnp.int32),
            vm((LEAVES, LEAF, RANK), BF),
            mats(31),
            mats(15),
            mats(8),
            mats(4),
            mats(2),
            mats(4),
            mats(6),
            vm((30, COLS, RANK), BF),
            vm((30, COLS, RANK), BF),
            vm((30, COLS, RANK), F32),
            vm((64, rows), BF),
            vm((64, rows), BF),
            vm((2 * GROUP, LEAF, LEAF), BF),
            vm((LEAVES, LEAF, LEAF), BF),
            vm((COLS, RANK), F32),
            vm((HALF, RANK), F32),
            vm((COLS, RANK), F32),
            vm((COLS, RANK), F32),
            vm((NZ, HALF, RANK), BF),
            vm((NX, COLS, RANK), BF),
            vm((COLS, RANK), F32),
            vm((4 * RANK, 2 * RANK), BF),
            vm((NZ * RANK, 2 * RANK), BF),
            vm((LEAVES * RANK, 3 * RANK), BF),
            vm((3 * RANK, 3 * RANK), BF),
            mats(6),
            vm((LEAVES, COLS, LEAF), BF),
            dma((16,)),
            dma((2,)),
            dma((2,)),
            dma((NZ - 1,)),
            dma((NZ - 1,)),
            dma((2 * (NX - 1),)),
            dma((2 * (NX - 1),)),
            dma((1,)),
            dma((1,)),
        ],
        compiler_params=pltpu.CompilerParams(
            collective_id=0, has_side_effects=True, vmem_limit_bytes=44 * 1024 * 1024
        ),
    )(*[pltpu.with_memory_space_constraint(arg, pltpu.HBM) for arg in args])
    return pl.pallas_call(
        finish,
        out_shape=jax.ShapeDtypeStruct((rows, COLS), F32),
        in_specs=[pl.BlockSpec(memory_space=vm)] * 5,
        out_specs=pl.BlockSpec(memory_space=pltpu.HBM),
        scratch_shapes=[vm((rows, COLS), F32), dma((LEAVES // 2,))],
        compiler_params=pltpu.CompilerParams(vmem_limit_bytes=16 * 1024 * 1024),
    )(*[pltpu.with_memory_space_constraint(part, vm) for part in parts])


def solution(mesh):
    placed = (
        P(None, "leaf"),
        P("leaf", "rhs"),
        P("leaf"),
        P("leaf", None, None),
        P("leaf", None, None),
        P("leaf", None, None),
        P(),
        P(),
    )
    return jax.shard_map(
        local, mesh=mesh, in_specs=placed, out_specs=P("leaf", "rhs"), check_vma=False
    )
```

```python
import functools
import math

import jax
import jax.numpy as jnp
from jax import lax
from jax.experimental import pallas as pl
from jax.experimental.pallas import tpu as pltpu
from jax.sharding import PartitionSpec as P

MESH = pl.DeviceIdType.MESH
BF, F32 = jnp.bfloat16, jnp.float32
LEAF, RANK, COLS, LEAVES = 256, 128, 128, 16
HALF = COLS // 2
NZ, NX = 8, 4
SCALE = math.sqrt(0.1 * math.log2(math.e))
GROUP = 4


def nn(a, b):
    return lax.dot_general(a, b, (((1,), (0,)), ((), ())), preferred_element_type=F32)


def nt(a, b):
    return lax.dot_general(a, b, (((1,), (1,)), ((), ())), preferred_element_type=F32)


def tn(a, b):
    return lax.dot_general(a, b, (((0,), (0,)), ((), ())), preferred_element_type=F32)


def split(u):
    hi = u.astype(BF)
    return hi, (u - hi.astype(F32)).astype(BF)


def beside(*parts):
    return jnp.concatenate(parts, axis=1)


def stacked(*parts):
    return jnp.concatenate(parts, axis=0)


def times(u, mat):
    return nn(beside(*u), stacked(mat, mat))


def times_t(u, mat):
    return nt(beside(*u), beside(mat, mat))


def mat_times(mat, u):
    both = nn(mat, beside(*u))
    return both[:, :RANK] + both[:, RANK:]


def kernel(
    points, charges, order, basis, trans, coup, top_t, top_c, near, bs_v, d0_v, h_v, ups,
    pts_v, q_v, ord_v, bas_v, tr_v, cp_v, t5_v, t6_v, t7_v, t8_v, c_v,
    uhi, ulo, side_v, lhs_v, rhs_v, e_v, pick_v,
    p_v, pp_v, u4_v, u4p_v, zbuf, xbuf, d5_v, g_v, q2_v, e0_v, src_v, m_v, qp_v,
    in_sem, cs_s, cs_r, zs, zr, xs, xr, ds_s, ds_r,
):
    me, col = lax.axis_index("leaf"), lax.axis_index("rhs")
    core = me % 2
    z = (me // 2) % NZ
    x = me // (2 * NZ)
    chip = me // 2

    def at(xx, zz, cc):
        return ((xx * NZ + zz) * 2 + cc, col)

    partner = at(x, z, 1 - core)
    zpeers = [at(x, (z + k) % NZ, core) for k in range(1, NZ)]
    xpeers = [at((x + k) % NX, z, cc) for k in range(1, NX) for cc in (core, 1 - core)]

    def load(src, dst, sem):
        cp = pltpu.make_async_copy(src, dst, in_sem.at[sem])
        cp.start()
        return cp

    barrier = pltpu.get_barrier_semaphore()
    peers = [zpeers[k] for k in (3, 2, 4, 1, 5)] + xpeers + [zpeers[0], zpeers[6], partner]
    for peer in peers[:5]:
        pl.semaphore_signal(barrier, inc=1, device_id=peer, device_id_type=MESH)

    order_cp = load(order, ord_v, 0)
    charges_cp = load(charges, q_v, 1)
    basis_cp = load(basis, bas_v, 2)
    trans_cp = load(trans, tr_v, 3)
    for peer in peers[5:]:
        pl.semaphore_signal(barrier, inc=1, device_id=peer, device_id_type=MESH)

    def span(leaf):
        return pl.ds(leaf * LEAF, LEAF)

    slot = lax.broadcasted_iota(jnp.int32, (LEAF, LEAF), 0)
    order_cp.wait()
    for leaf in range(LEAVES):
        where = ord_v[span(leaf)] & (LEAF - 1)
        pick_v[leaf] = jnp.where(slot == where[None, :], 1.0, 0.0).astype(BF)
    charges_cp.wait()
    for leaf in range(LEAVES):
        qp_v[leaf] = tn(q_v[span(leaf)], pick_v[leaf]).astype(BF)
    basis_cp.wait()

    def put(node, u):
        uhi[node], ulo[node] = split(u)

    def read(node):
        return uhi[node], ulo[node]

    def parent(left, right, mats):
        mats = mats.reshape(2 * RANK, RANK)
        return nn(beside(left[0], right[0]), mats) + nn(beside(left[1], right[1]), mats)

    def raise_level(start, count):
        for i in range(count // 2):
            low = start + 2 * i
            put(start + count + i, parent(read(low), read(low + 1), tr_v[low : low + 2]))

    for leaf in range(LEAVES):
        put(leaf, nn(qp_v[leaf], bas_v[leaf]))
    trans_cp.wait()

    root = tr_v[30]
    paths = [split(nn(tr_v[28 + i], root)) for i in range(2)]
    raise_level(0, 16)
    for i in range(4):
        hi, lo = split(mat_times(tr_v[24 + i], paths[i // 2]))
        g_v[i * RANK : (i + 1) * RANK, :] = beside(hi, lo)
    raise_level(16, 8)
    both = nn(beside(*[uhi[24 + i] for i in range(4)]), g_v[...])
    p_v[...] = both[:, :RANK] + both[:, RANK:] + nn(beside(*[ulo[24 + i] for i in range(4)]), g_v[:, :RANK])

    pl.semaphore_wait(barrier, len(peers))
    mine_rows = pl.ds(pl.multiple_of(core * HALF, HALF), HALF)
    other_rows = pl.ds(pl.multiple_of((1 - core) * HALF, HALF), HALF)

    def remote(src, dst, send, recv, peer):
        return pltpu.make_async_remote_copy(
            src_ref=src, dst_ref=dst, send_sem=send, recv_sem=recv, device_id=peer, device_id_type=MESH
        )

    swap = remote(p_v.at[other_rows], pp_v, cs_s.at[0], cs_r.at[0], partner)
    swap.start()
    swap.wait_recv()
    zbuf[z] = (p_v[mine_rows] + pp_v[...]).astype(BF)
    zsends = [remote(zbuf.at[z], zbuf.at[z], zs.at[k], zr.at[k], zpeers[k]) for k in range(NZ - 1)]
    for k in (3, 4, 2, 5, 1, 6, 0):
        zsends[k].start()

    late = [
        load(points, pts_v, 4),
        load(top_t.at[pl.ds(x * 8, 8)], t5_v, 5),
        load(top_t.at[pl.ds(32 + x * 4, 4)], t6_v, 6),
        load(top_t.at[pl.ds(48 + x * 2, 2)], t7_v, 7),
        load(top_t.at[pl.ds(56, 4)], t8_v, 8),
        load(top_c.at[chip], c_v.at[0], 9),
        load(top_c.at[32 + chip // 2], c_v.at[1], 10),
        load(top_c.at[48 + chip // 4], c_v.at[2], 11),
        load(top_c.at[56 + x], c_v.at[3], 12),
        load(top_c.at[60 + x // 2], c_v.at[4], 13),
        load(top_c.at[62], c_v.at[5], 14),
        load(coup, cp_v, 15),
    ]

    raise_level(24, 4)
    u4_v[...] = parent(read(28), read(29), tr_v[28:30])
    swap4 = remote(u4_v, u4p_v, cs_s.at[1], cs_r.at[1], partner)
    for cp in late:
        cp.wait()

    t67 = [split(nn(t6_v[i], t7_v[i // 2])) for i in range(4)]

    xs_all = pts_v[...] * SCALE
    h = xs_all.astype(BF).astype(F32)
    rest = xs_all - h
    m = rest.astype(BF).astype(F32)
    low = rest - m
    norm = jnp.sum(xs_all * xs_all, axis=0, keepdims=True)
    nh = norm.astype(BF).astype(F32)
    nrest = norm - nh
    nm = nrest.astype(BF).astype(F32)
    nl = nrest - nm
    wide = norm.shape[1]
    one = jnp.ones((1, wide), F32)
    zero = jnp.zeros((2, wide), F32)
    pad = jnp.zeros((8, wide), F32)
    lhs_v[...] = stacked(h, h, m, m, h, low, nh, nm, nl, one, one, one, zero, pad).astype(BF)
    rhs_v[...] = stacked(2 * h, 2 * m, 2 * h, 2 * m, 2 * low, 2 * h, -one, -one, -one, -nh, -nm, -nl, zero, pad).astype(BF)

    for i in range(NZ):
        hi, lo = split(mat_times(t5_v[i], t67[i // 2]))
        q2_v[i * RANK : (i + 1) * RANK, :] = beside(hi, lo)

    def towards(index, bit):
        mat = c_v[index]
        return jnp.where(bit == 0, mat.astype(F32).T, mat.astype(F32)).astype(BF)

    for i, bit in enumerate((core, z % 2, (z // 2) % 2, z // 4, x % 2, x // 2)):
        m_v[i] = towards(i, bit)

    def blocks(leaves):
        for leaf in leaves:
            where = span(leaf)
            e_v[leaf % (2 * GROUP)] = jnp.exp2(tn(lhs_v[:, where], rhs_v[:, where])).astype(BF)

    def direct(leaves):
        for leaf in leaves:
            q = q_v[span(leaf)]
            near[span(leaf), :] = nn(e_v[leaf % (2 * GROUP)], q) + 0.5 * q.astype(F32)

    far = 2 - 2 * (x // 2)
    own_path = pl.ds(pl.multiple_of(z * RANK, RANK), RANK)
    blocks(range(GROUP))
    down_path = [split(mat_times(root, (q2_v[own_path, :RANK], q2_v[own_path, RANK:])))]
    from_far = split(nn(m_v[5], t8_v[x].astype(F32).T.astype(BF)))
    across = []
    for group, start in ((0, 28), (1, 24), (2, 16), (3, 0)):
        if group < 3:
            blocks(range((group + 1) * GROUP, (group + 2) * GROUP))
        count = 2 * len(down_path)
        down_path = [split(mat_times(tr_v[start + i], down_path[i // 2])) for i in range(count)]
        if group == 0:
            across = [split(mat_times(t8_v[far + i], from_far)) for i in range(2)]
        direct(range(group * GROUP, (group + 1) * GROUP))
    for i in range(LEAVES):
        hi, lo = down_path[i]
        e0_v[i * RANK : (i + 1) * RANK, :] = beside(hi, lo, hi)
    src_v[...] = stacked(
        beside(m_v[4], m_v[4], jnp.zeros((RANK, RANK), BF)),
        beside(across[0][0], across[0][0], across[0][1]),
        beside(across[1][0], across[1][0], across[1][1]),
    )
    swap4.start()
    for leaf in range(LEAVES):
        bs_v[leaf] = nn(pick_v[leaf], bas_v[leaf]).astype(BF)
    for pair in range(15):
        mat = cp_v[pair]
        side_v[2 * pair] = times_t(read(2 * pair + 1), mat)
        side_v[2 * pair + 1] = times(read(2 * pair), mat)

    for cp in zsends:
        cp.wait_recv()
    u8 = nn(beside(*[zbuf[i] for i in range(NZ)]), q2_v[...])
    xbuf[x, mine_rows] = (u8[:, :RANK] + u8[:, RANK:]).astype(BF)
    xsends = [
        remote(xbuf.at[x, mine_rows], xbuf.at[x, mine_rows], xs.at[k], xr.at[k], xpeers[k])
        for k in range(2 * (NX - 1))
    ]
    for k in (2, 3, 0, 1, 4, 5):
        xsends[k].start()

    def sibling(i):
        return i + 1 - 2 * (i % 2)

    def level6(i):
        return split(nn(beside(zbuf[2 * i], zbuf[2 * i + 1]), stacked(t5_v[2 * i], t5_v[2 * i + 1])))

    half_z, quarter_z = z // 2, z // 4
    other = 1 - quarter_z
    next6, pair6 = level6(sibling(half_z)), (level6(2 * other), level6(2 * other + 1))
    side5 = nn(zbuf[sibling(z)], m_v[1])
    next7 = split(times(pair6[0], t6_v[2 * other]) + times(pair6[1], t6_v[2 * other + 1]))
    side6 = times(next6, m_v[2])
    d7 = times(next7, m_v[3])
    d6 = side6 + times_t(split(d7), t6_v[half_z])
    d5_v[mine_rows] = side5 + times_t(split(d6), t5_v[z])
    back = remote(d5_v.at[mine_rows], d5_v.at[mine_rows], ds_s.at[0], ds_r.at[0], partner)
    back.start()
    for i in range(LEAVES // 2):
        where = slice(2 * i * RANK, 2 * (i + 1) * RANK)
        hi, lo = split(nt(src_v[...], e0_v[where]))
        h_v[: 3 * RANK, where] = hi
        h_v[3 * RANK :, where] = lo
    swap4.wait_recv()
    side4 = times(split(u4p_v[...]), m_v[0])
    back.wait_recv()
    down = [split(side4 + times_t(split(d5_v[...]), root))]
    for start, count in ((28, 2), (24, 4), (16, 8)):
        down = [split(side_v[start + i] + times_t(down[i // 2], tr_v[start + i])) for i in range(count)]
    for i in range(LEAVES):
        d0_v[i] = side_v[i] + times_t(down[i // 2], tr_v[i])

    for cp in [swap, swap4, back] + zsends + xsends:
        cp.wait_send()
    for cp in xsends:
        cp.wait_recv()
    ups[...] = beside(xbuf[sibling(x)], xbuf[far], xbuf[far + 1])


def finish(near, bs_v, d0_v, h_v, ups, out, sum_v, sem):
    u8s = beside(ups[...], ups[...])
    pairs = LEAVES // 2
    tops, downs, copies = {}, {}, []

    def final(i):
        for leaf in (2 * i, 2 * i + 1):
            where = pl.ds(leaf * LEAF, LEAF)
            own = bs_v[leaf]
            sum_v[where] = near[where] + nt(beside(own, own), beside(*downs[leaf]))
        where = pl.ds(2 * i * LEAF, 2 * LEAF)
        copies.append(pltpu.make_async_copy(sum_v.at[where], out.at[where], sem.at[i]))
        copies[-1].start()

    for step in range(pairs + 2):
        if step < pairs:
            tops[step] = nn(u8s, h_v[:, 2 * step * RANK : 2 * (step + 1) * RANK])
        if 1 <= step <= pairs:
            for j in range(2):
                leaf = 2 * (step - 1) + j
                downs[leaf] = split(d0_v[leaf] + tops[step - 1][:, j * RANK : (j + 1) * RANK])
        if step >= 2:
            final(step - 2)
    for cp in copies:
        cp.wait()


def local(*args):
    vm = pltpu.VMEM
    dma = pltpu.SemaphoreType.DMA
    rows = LEAVES * LEAF
    mats = lambda n: vm((n, RANK, RANK), BF)
    parts = pl.pallas_call(
        kernel,
        out_shape=(
            vm((rows, COLS), F32),
            vm((LEAVES, LEAF, RANK), BF),
            vm((LEAVES, COLS, RANK), F32),
            vm((6 * RANK, LEAVES * RANK), BF),
            vm((COLS, 3 * RANK), BF),
        ),
        in_specs=[pl.BlockSpec(memory_space=pltpu.HBM)] * 8,
        out_specs=[pl.BlockSpec(memory_space=vm)] * 5,
        scratch_shapes=[
            vm((8, rows), F32),
            vm((rows, COLS), BF),
            vm((rows,), jnp.int32),
            vm((LEAVES, LEAF, RANK), BF),
            mats(31),
            mats(15),
            mats(8),
            mats(4),
            mats(2),
            mats(4),
            mats(6),
            vm((30, COLS, RANK), BF),
            vm((30, COLS, RANK), BF),
            vm((30, COLS, RANK), F32),
            vm((64, rows), BF),
            vm((64, rows), BF),
            vm((2 * GROUP, LEAF, LEAF), BF),
            vm((LEAVES, LEAF, LEAF), BF),
            vm((COLS, RANK), F32),
            vm((HALF, RANK), F32),
            vm((COLS, RANK), F32),
            vm((COLS, RANK), F32),
            vm((NZ, HALF, RANK), BF),
            vm((NX, COLS, RANK), BF),
            vm((COLS, RANK), F32),
            vm((4 * RANK, 2 * RANK), BF),
            vm((NZ * RANK, 2 * RANK), BF),
            vm((LEAVES * RANK, 3 * RANK), BF),
            vm((3 * RANK, 3 * RANK), BF),
            mats(6),
            vm((LEAVES, COLS, LEAF), BF),
            dma((16,)),
            dma((2,)),
            dma((2,)),
            dma((NZ - 1,)),
            dma((NZ - 1,)),
            dma((2 * (NX - 1),)),
            dma((2 * (NX - 1),)),
            dma((1,)),
            dma((1,)),
        ],
        compiler_params=pltpu.CompilerParams(
            collective_id=0, has_side_effects=True, vmem_limit_bytes=44 * 1024 * 1024
        ),
    )(*[pltpu.with_memory_space_constraint(arg, pltpu.HBM) for arg in args])
    return pl.pallas_call(
        finish,
        out_shape=jax.ShapeDtypeStruct((rows, COLS), F32),
        in_specs=[pl.BlockSpec(memory_space=vm)] * 5,
        out_specs=pl.BlockSpec(memory_space=pltpu.HBM),
        scratch_shapes=[vm((rows, COLS), F32), dma((LEAVES // 2,))],
        compiler_params=pltpu.CompilerParams(vmem_limit_bytes=16 * 1024 * 1024),
    )(*[pltpu.with_memory_space_constraint(part, vm) for part in parts])


def solution(mesh):
    placed = (
        P(None, "leaf"),
        P("leaf", "rhs"),
        P("leaf"),
        P("leaf", None, None),
        P("leaf", None, None),
        P("leaf", None, None),
        P(),
        P(),
    )
    return jax.shard_map(
        local, mesh=mesh, in_specs=placed, out_specs=P("leaf", "rhs"), check_vma=False
    )
```

```python
import functools
import math

import jax
import jax.numpy as jnp
from jax import lax
from jax.experimental import pallas as pl
from jax.experimental.pallas import tpu as pltpu
from jax.sharding import PartitionSpec as P

MESH = pl.DeviceIdType.MESH
BF, F32 = jnp.bfloat16, jnp.float32
LEAF, RANK, COLS, LEAVES = 256, 128, 128, 16
HALF = COLS // 2
NZ, NX = 8, 4
SCALE = math.sqrt(0.1 * math.log2(math.e))
GROUP = 4


def nn(a, b):
    return lax.dot_general(a, b, (((1,), (0,)), ((), ())), preferred_element_type=F32)


def nt(a, b):
    return lax.dot_general(a, b, (((1,), (1,)), ((), ())), preferred_element_type=F32)


def tn(a, b):
    return lax.dot_general(a, b, (((0,), (0,)), ((), ())), preferred_element_type=F32)


def split(u):
    hi = u.astype(BF)
    return hi, (u - hi.astype(F32)).astype(BF)


def beside(*parts):
    return jnp.concatenate(parts, axis=1)


def stacked(*parts):
    return jnp.concatenate(parts, axis=0)


def times(u, mat):
    return nn(beside(*u), stacked(mat, mat))


def times_t(u, mat):
    return nt(beside(*u), beside(mat, mat))


def mat_times(mat, u):
    both = nn(mat, beside(*u))
    return both[:, :RANK] + both[:, RANK:]


def kernel(
    points, charges, order, basis, trans, coup, top_t, top_c, near, bs_v, h_v, ups,
    pts_v, q_v, ord_v, bas_v, tr_v, cp_v, t5_v, t6_v, t7_v, t8_v, c_v,
    uhi, ulo, side_v, lhs_v, rhs_v, e_v, pick_v,
    p_v, pp_v, u4_v, u4p_v, zbuf, xbuf, d5_v, g_v, q2_v, e0_v, src_v, m_v, qp_v,
    in_sem, cs_s, cs_r, zs, zr, xs, xr, ds_s, ds_r,
):
    me, col = lax.axis_index("leaf"), lax.axis_index("rhs")
    core = me % 2
    z = (me // 2) % NZ
    x = me // (2 * NZ)
    chip = me // 2

    def at(xx, zz, cc):
        return ((xx * NZ + zz) * 2 + cc, col)

    partner = at(x, z, 1 - core)
    zpeers = [at(x, (z + k) % NZ, core) for k in range(1, NZ)]
    xpeers = [at((x + k) % NX, z, cc) for k in range(1, NX) for cc in (core, 1 - core)]

    def load(src, dst, sem):
        cp = pltpu.make_async_copy(src, dst, in_sem.at[sem])
        cp.start()
        return cp

    barrier = pltpu.get_barrier_semaphore()
    peers = [zpeers[k] for k in (3, 2, 4, 1, 5)] + xpeers + [zpeers[0], zpeers[6], partner]
    for peer in peers[:5]:
        pl.semaphore_signal(barrier, inc=1, device_id=peer, device_id_type=MESH)

    order_cp = load(order, ord_v, 0)
    charges_cp = load(charges, q_v, 1)
    basis_cp = load(basis, bas_v, 2)
    trans_cp = load(trans, tr_v, 3)
    for peer in peers[5:]:
        pl.semaphore_signal(barrier, inc=1, device_id=peer, device_id_type=MESH)

    def span(leaf):
        return pl.ds(leaf * LEAF, LEAF)

    slot = lax.broadcasted_iota(jnp.int32, (LEAF, LEAF), 0)
    order_cp.wait()
    for leaf in range(LEAVES):
        where = ord_v[span(leaf)] & (LEAF - 1)
        pick_v[leaf] = jnp.where(slot == where[None, :], 1.0, 0.0).astype(BF)
    charges_cp.wait()
    for leaf in range(LEAVES):
        qp_v[leaf] = tn(q_v[span(leaf)], pick_v[leaf]).astype(BF)
    basis_cp.wait()

    def put(node, u):
        uhi[node], ulo[node] = split(u)

    def read(node):
        return uhi[node], ulo[node]

    def parent(left, right, mats):
        mats = mats.reshape(2 * RANK, RANK)
        return nn(beside(left[0], right[0]), mats) + nn(beside(left[1], right[1]), mats)

    def raise_level(start, count):
        for i in range(count // 2):
            low = start + 2 * i
            put(start + count + i, parent(read(low), read(low + 1), tr_v[low : low + 2]))

    for leaf in range(LEAVES):
        put(leaf, nn(qp_v[leaf], bas_v[leaf]))
    trans_cp.wait()

    root = tr_v[30]
    paths = [split(nn(tr_v[28 + i], root)) for i in range(2)]
    raise_level(0, 16)
    for i in range(4):
        hi, lo = split(mat_times(tr_v[24 + i], paths[i // 2]))
        g_v[i * RANK : (i + 1) * RANK, :] = beside(hi, lo)
    raise_level(16, 8)
    both = nn(beside(*[uhi[24 + i] for i in range(4)]), g_v[...])
    p_v[...] = both[:, :RANK] + both[:, RANK:] + nn(beside(*[ulo[24 + i] for i in range(4)]), g_v[:, :RANK])

    pl.semaphore_wait(barrier, len(peers))
    mine_rows = pl.ds(pl.multiple_of(core * HALF, HALF), HALF)
    other_rows = pl.ds(pl.multiple_of((1 - core) * HALF, HALF), HALF)

    def remote(src, dst, send, recv, peer):
        return pltpu.make_async_remote_copy(
            src_ref=src, dst_ref=dst, send_sem=send, recv_sem=recv, device_id=peer, device_id_type=MESH
        )

    swap = remote(p_v.at[other_rows], pp_v, cs_s.at[0], cs_r.at[0], partner)
    swap.start()
    swap.wait_recv()
    zbuf[z] = (p_v[mine_rows] + pp_v[...]).astype(BF)
    zsends = [remote(zbuf.at[z], zbuf.at[z], zs.at[k], zr.at[k], zpeers[k]) for k in range(NZ - 1)]
    for k in (3, 4, 2, 5, 1, 6, 0):
        zsends[k].start()

    late = [
        load(points, pts_v, 4),
        load(top_t.at[pl.ds(x * 8, 8)], t5_v, 5),
        load(top_t.at[pl.ds(32 + x * 4, 4)], t6_v, 6),
        load(top_t.at[pl.ds(48 + x * 2, 2)], t7_v, 7),
        load(top_t.at[pl.ds(56, 4)], t8_v, 8),
        load(top_c.at[chip], c_v.at[0], 9),
        load(top_c.at[32 + chip // 2], c_v.at[1], 10),
        load(top_c.at[48 + chip // 4], c_v.at[2], 11),
        load(top_c.at[56 + x], c_v.at[3], 12),
        load(top_c.at[60 + x // 2], c_v.at[4], 13),
        load(top_c.at[62], c_v.at[5], 14),
        load(coup, cp_v, 15),
    ]

    raise_level(24, 4)
    u4_v[...] = parent(read(28), read(29), tr_v[28:30])
    swap4 = remote(u4_v, u4p_v, cs_s.at[1], cs_r.at[1], partner)
    for cp in late:
        cp.wait()

    t67 = [split(nn(t6_v[i], t7_v[i // 2])) for i in range(4)]

    xs_all = pts_v[...] * SCALE
    h = xs_all.astype(BF).astype(F32)
    rest = xs_all - h
    m = rest.astype(BF).astype(F32)
    low = rest - m
    norm = jnp.sum(xs_all * xs_all, axis=0, keepdims=True)
    nh = norm.astype(BF).astype(F32)
    nrest = norm - nh
    nm = nrest.astype(BF).astype(F32)
    nl = nrest - nm
    wide = norm.shape[1]
    one = jnp.ones((1, wide), F32)
    zero = jnp.zeros((2, wide), F32)
    pad = jnp.zeros((8, wide), F32)
    lhs_v[...] = stacked(h, h, m, m, h, low, nh, nm, nl, one, one, one, zero, pad).astype(BF)
    rhs_v[...] = stacked(2 * h, 2 * m, 2 * h, 2 * m, 2 * low, 2 * h, -one, -one, -one, -nh, -nm, -nl, zero, pad).astype(BF)

    for i in range(NZ):
        hi, lo = split(mat_times(t5_v[i], t67[i // 2]))
        q2_v[i * RANK : (i + 1) * RANK, :] = beside(hi, lo)

    def towards(index, bit):
        mat = c_v[index]
        return jnp.where(bit == 0, mat.astype(F32).T, mat.astype(F32)).astype(BF)

    for i, bit in enumerate((core, z % 2, (z // 2) % 2, z // 4, x % 2, x // 2)):
        m_v[i] = towards(i, bit)

    def blocks(leaves):
        for leaf in leaves:
            where = span(leaf)
            e_v[leaf % (2 * GROUP)] = jnp.exp2(tn(lhs_v[:, where], rhs_v[:, where])).astype(BF)

    def direct(leaves):
        for leaf in leaves:
            q = q_v[span(leaf)]
            near[span(leaf), :] = nn(e_v[leaf % (2 * GROUP)], q) + 0.5 * q.astype(F32)

    far = 2 - 2 * (x // 2)
    own_path = pl.ds(pl.multiple_of(z * RANK, RANK), RANK)
    blocks(range(GROUP))
    down_path = [split(mat_times(root, (q2_v[own_path, :RANK], q2_v[own_path, RANK:])))]
    from_far = split(nn(m_v[5], t8_v[x].astype(F32).T.astype(BF)))
    across = []
    for group, start in ((0, 28), (1, 24), (2, 16), (3, 0)):
        if group < 3:
            blocks(range((group + 1) * GROUP, (group + 2) * GROUP))
        count = 2 * len(down_path)
        down_path = [split(mat_times(tr_v[start + i], down_path[i // 2])) for i in range(count)]
        if group == 0:
            across = [split(mat_times(t8_v[far + i], from_far)) for i in range(2)]
        direct(range(group * GROUP, (group + 1) * GROUP))
    for i in range(LEAVES):
        hi, lo = down_path[i]
        e0_v[i * RANK : (i + 1) * RANK, :] = beside(hi, lo, hi)
    src_v[...] = stacked(
        beside(m_v[4], m_v[4], jnp.zeros((RANK, RANK), BF)),
        beside(across[0][0], across[0][0], across[0][1]),
        beside(across[1][0], across[1][0], across[1][1]),
    )
    swap4.start()
    for leaf in range(LEAVES):
        bs_v[leaf] = nn(pick_v[leaf], bas_v[leaf]).astype(BF)
    for pair in range(15):
        mat = cp_v[pair]
        side_v[2 * pair] = times_t(read(2 * pair + 1), mat)
        side_v[2 * pair + 1] = times(read(2 * pair), mat)

    for cp in zsends:
        cp.wait_recv()
    u8 = nn(beside(*[zbuf[i] for i in range(NZ)]), q2_v[...])
    xbuf[x, mine_rows] = (u8[:, :RANK] + u8[:, RANK:]).astype(BF)
    xsends = [
        remote(xbuf.at[x, mine_rows], xbuf.at[x, mine_rows], xs.at[k], xr.at[k], xpeers[k])
        for k in range(2 * (NX - 1))
    ]
    for k in (2, 3, 0, 1, 4, 5):
        xsends[k].start()

    def sibling(i):
        return i + 1 - 2 * (i % 2)

    def level6(i):
        return split(nn(beside(zbuf[2 * i], zbuf[2 * i + 1]), stacked(t5_v[2 * i], t5_v[2 * i + 1])))

    half_z, quarter_z = z // 2, z // 4
    other = 1 - quarter_z
    next6, pair6 = level6(sibling(half_z)), (level6(2 * other), level6(2 * other + 1))
    side5 = nn(zbuf[sibling(z)], m_v[1])
    next7 = split(times(pair6[0], t6_v[2 * other]) + times(pair6[1], t6_v[2 * other + 1]))
    side6 = times(next6, m_v[2])
    d7 = times(next7, m_v[3])
    d6 = side6 + times_t(split(d7), t6_v[half_z])
    d5_v[mine_rows] = side5 + times_t(split(d6), t5_v[z])
    back = remote(d5_v.at[mine_rows], d5_v.at[mine_rows], ds_s.at[0], ds_r.at[0], partner)
    back.start()
    for i in range(LEAVES // 2):
        where = slice(2 * i * RANK, 2 * (i + 1) * RANK)
        hi, lo = split(nt(src_v[...], e0_v[where]))
        h_v[: 3 * RANK, where] = hi
        h_v[3 * RANK :, where] = lo
    swap4.wait_recv()
    side4 = times(split(u4p_v[...]), m_v[0])
    back.wait_recv()
    down = [split(side4 + times_t(split(d5_v[...]), root))]
    for start, count in ((28, 2), (24, 4), (16, 8)):
        down = [split(side_v[start + i] + times_t(down[i // 2], tr_v[start + i])) for i in range(count)]
    for i in range(LEAVES):
        uhi[i], ulo[i] = split(side_v[i] + times_t(down[i // 2], tr_v[i]))
    for i in range(LEAVES):
        near[span(i), :] += nt(beside(bs_v[i], bs_v[i]), beside(uhi[i], ulo[i]))

    for cp in [swap, swap4, back] + zsends + xsends:
        cp.wait_send()
    for cp in xsends:
        cp.wait_recv()
    ups[...] = beside(xbuf[sibling(x)], xbuf[far], xbuf[far + 1])


def finish(near, bs_v, h_v, ups, out, sum_v, sem):
    u8s = beside(ups[...], ups[...])
    pairs = LEAVES // 2
    tops, downs, copies = {}, {}, []

    def final(i):
        for leaf in (2 * i, 2 * i + 1):
            where = pl.ds(leaf * LEAF, LEAF)
            own = bs_v[leaf]
            sum_v[where] = near[where] + nt(beside(own, own), beside(*downs[leaf]))
        where = pl.ds(2 * i * LEAF, 2 * LEAF)
        copies.append(pltpu.make_async_copy(sum_v.at[where], out.at[where], sem.at[i]))
        copies[-1].start()

    for step in range(pairs + 2):
        if step < pairs:
            tops[step] = nn(u8s, h_v[:, 2 * step * RANK : 2 * (step + 1) * RANK])
        if 1 <= step <= pairs:
            for j in range(2):
                leaf = 2 * (step - 1) + j
                downs[leaf] = split(tops[step - 1][:, j * RANK : (j + 1) * RANK])
        if step >= 2:
            final(step - 2)
    for cp in copies:
        cp.wait()


def local(*args):
    vm = pltpu.VMEM
    dma = pltpu.SemaphoreType.DMA
    rows = LEAVES * LEAF
    mats = lambda n: vm((n, RANK, RANK), BF)
    parts = pl.pallas_call(
        kernel,
        out_shape=(
            vm((rows, COLS), F32),
            vm((LEAVES, LEAF, RANK), BF),
            vm((6 * RANK, LEAVES * RANK), BF),
            vm((COLS, 3 * RANK), BF),
        ),
        in_specs=[pl.BlockSpec(memory_space=pltpu.HBM)] * 8,
        out_specs=[pl.BlockSpec(memory_space=vm)] * 4,
        scratch_shapes=[
            vm((8, rows), F32),
            vm((rows, COLS), BF),
            vm((rows,), jnp.int32),
            vm((LEAVES, LEAF, RANK), BF),
            mats(31),
            mats(15),
            mats(8),
            mats(4),
            mats(2),
            mats(4),
            mats(6),
            vm((30, COLS, RANK), BF),
            vm((30, COLS, RANK), BF),
            vm((30, COLS, RANK), F32),
            vm((64, rows), BF),
            vm((64, rows), BF),
            vm((2 * GROUP, LEAF, LEAF), BF),
            vm((LEAVES, LEAF, LEAF), BF),
            vm((COLS, RANK), F32),
            vm((HALF, RANK), F32),
            vm((COLS, RANK), F32),
            vm((COLS, RANK), F32),
            vm((NZ, HALF, RANK), BF),
            vm((NX, COLS, RANK), BF),
            vm((COLS, RANK), F32),
            vm((4 * RANK, 2 * RANK), BF),
            vm((NZ * RANK, 2 * RANK), BF),
            vm((LEAVES * RANK, 3 * RANK), BF),
            vm((3 * RANK, 3 * RANK), BF),
            mats(6),
            vm((LEAVES, COLS, LEAF), BF),
            dma((16,)),
            dma((2,)),
            dma((2,)),
            dma((NZ - 1,)),
            dma((NZ - 1,)),
            dma((2 * (NX - 1),)),
            dma((2 * (NX - 1),)),
            dma((1,)),
            dma((1,)),
        ],
        compiler_params=pltpu.CompilerParams(
            collective_id=0, has_side_effects=True, vmem_limit_bytes=44 * 1024 * 1024
        ),
    )(*[pltpu.with_memory_space_constraint(arg, pltpu.HBM) for arg in args])
    return pl.pallas_call(
        finish,
        out_shape=jax.ShapeDtypeStruct((rows, COLS), F32),
        in_specs=[pl.BlockSpec(memory_space=vm)] * 4,
        out_specs=pl.BlockSpec(memory_space=pltpu.HBM),
        scratch_shapes=[vm((rows, COLS), F32), dma((LEAVES // 2,))],
        compiler_params=pltpu.CompilerParams(vmem_limit_bytes=16 * 1024 * 1024),
    )(*[pltpu.with_memory_space_constraint(part, vm) for part in parts])


def solution(mesh):
    placed = (
        P(None, "leaf"),
        P("leaf", "rhs"),
        P("leaf"),
        P("leaf", None, None),
        P("leaf", None, None),
        P("leaf", None, None),
        P(),
        P(),
    )
    return jax.shard_map(
        local, mesh=mesh, in_specs=placed, out_specs=P("leaf", "rhs"), check_vma=False
    )
```
